32 devices in a mesh: groups: 2 (over x), blk: 16 (over z, y, core).
Axes of the slice: x: 2, y: 2, z: 4, core: 2. Of those that a mesh axis runs over, the one named last changes fastest.
Arguments:
- attn: bfloat16 [8192, 3072], P(('groups', 'blk')), parts along dimension 0, may hold values from -6 to 6
- resid: bfloat16 [8192, 3072], P(('groups', 'blk')), parts along dimension 0, may hold values from -6 to 6
- frozen: bfloat16 [3072, 3072], P('blk'), may hold values from -0.109375 to 0.109375
- adapter_down_weight: float32 [3072, 64], replicated, may hold values from -0.109375 to 0.109375
- adapter_up_weight: float32 [64, 3072], replicated, may hold values from -0.109375 to 0.109375
- timestep_gate: float32 [50, 3072], replicated, may hold values from 0.25 to 1.5
- guidance_gate: float32 [16, 3072], replicated, may hold values from -0.5 to 0.5
- timestep_index: int32 [2], P('groups'), parts along dimension 0, may hold values from 0 to 49
- guidance_index: int32 [2], P('groups'), parts along dimension 0, may hold values from 0 to 15
- cotangent: bfloat16 [8192, 3072], P(('groups', 'blk')), parts along dimension 0, may hold values from -6 to 6
Outputs:
- updated: bfloat16 [8192, 3072], P(('groups', 'blk')), parts along dimension 0
- grad_attn: bfloat16 [8192, 3072], P(('groups', 'blk')), parts along dimension 0
- grad_down: float32 [6144, 64], P(('groups', 'blk')), parts along dimension 0
- grad_up_t: float32 [6144, 64], P(('groups', 'blk')), parts along dimension 0
The draws below stay inside these ranges and needn't reach their ends.
There are 2 independent parts, one for each index of `groups`. The reference program is written for one: setup_inputs(seed, part) draws one part's arguments, and reference() takes and returns one part's arrays. A program takes and returns all parts, laid end to end along the dimension named above; an argument that names none is the same for every part. Nothing has to cross between parts.
All inputs are finite; a program needn't handle non-finite values.
Results may differ from the reference program's by a relative error of at most 0.0059.
Values may be sent and summed in bfloat16 or wider, within the bound.
No kernel may reach another device: no remote copies, remote signals or barrier semaphores. Data moves between devices by JAX's collectives and lax.ppermute only.
A program may use at most 128 MiB of HBM per device.

```python
import jax
import jax.numpy as jnp

MODEL_WIDTH = 3072
ADAPTER_RANK = 64
IMAGE_TOKENS = 4096
NT = 50
NG = 16
TOKENS = 4096
SAMPLES = 1


def strengthened(result, own_key, source, target, blocks, factor):
    def block_of(axis_at):
        return (jnp.arange(result.shape[axis_at]) // (result.shape[axis_at] // blocks)).reshape((-1,) + (1,) * (result.ndim - 1 - axis_at))

    near = jax.random.permutation(own_key, blocks)[block_of(target)]
    far = (block_of(target) + blocks // 2) % blocks
    return jnp.where((block_of(source) == near) | (block_of(source) == far), factor * result, result)


def steps_of(stream_key, extent, split, least, largest):
    level = 1.0
    for dim, parts in split:
        draws = jax.random.uniform(jax.random.fold_in(jax.random.fold_in(stream_key, 6), dim), (parts,), jnp.float32, least / len(split), largest / len(split))
        level = level * jnp.repeat(jnp.exp(draws), extent[dim] // parts).reshape((-1,) + (1,) * (len(extent) - 1 - dim))
    return level


def scatter_about(own_key, shape, deviation, most, cuts=(), dtype=jnp.bfloat16):
    entries = deviation * jax.random.normal(own_key, shape, jnp.float32)
    if cuts:
        entries = entries * steps_of(own_key, shape, cuts, -0.22, 0.18)
    return jnp.clip(entries, -most, most).astype(dtype)


def heavy_noise(rng, extent, width, most, cuts, heavy, kind=jnp.bfloat16):
    array = width * jax.random.normal(rng, extent, jnp.float32)
    if cuts:
        array = array * steps_of(rng, extent, cuts, -0.22, 0.18)
    return jnp.clip(strengthened(array, jax.random.fold_in(rng, 3), *heavy), -most, most).astype(kind)


def setup_inputs(seed: int = 0, part: int = 0) -> dict:
    key_list = jax.random.split(jax.random.key(seed), 11)
    own_keys = jax.random.split(jax.random.fold_in(key_list[10], part), 11)
    attn = heavy_noise(own_keys[0], (TOKENS, MODEL_WIDTH), 1.0, 6.0, ((0, 16),), (0, 1, 16, 2.0))
    resid = scatter_about(own_keys[1], (TOKENS, MODEL_WIDTH), 1.0, 6.0, ((0, 16),))
    frozen = scatter_about(key_list[2], (MODEL_WIDTH, MODEL_WIDTH), MODEL_WIDTH ** -0.5, 0.109375, ((0, 16),))
    adapter_down_weight = scatter_about(key_list[3], (MODEL_WIDTH, ADAPTER_RANK), MODEL_WIDTH ** -0.5, 0.109375, (), jnp.float32)
    adapter_up_weight = scatter_about(key_list[4], (ADAPTER_RANK, MODEL_WIDTH), MODEL_WIDTH ** -0.5, 0.109375, (), jnp.float32)
    timestep_gate = jnp.clip(jax.random.uniform(key_list[5], (NT, MODEL_WIDTH), jnp.float32, 0.25, 1.5), 0.25, 1.5)
    guidance_gate = jnp.clip(jax.random.uniform(key_list[6], (NG, MODEL_WIDTH), jnp.float32, -0.5, 0.5), -0.5, 0.5)
    timestep_index = jax.random.randint(own_keys[7], (SAMPLES,), 0, NT).astype(jnp.int32)
    guidance_index = jax.random.randint(own_keys[8], (SAMPLES,), 0, NG).astype(jnp.int32)
    cotangent = heavy_noise(own_keys[9], (TOKENS, MODEL_WIDTH), 1.0, 6.0, ((0, 16),), (0, 1, 16, 2.0))
    return dict(attn=attn, resid=resid, frozen=frozen, adapter_down_weight=adapter_down_weight, adapter_up_weight=adapter_up_weight, timestep_gate=timestep_gate, guidance_gate=guidance_gate, timestep_index=timestep_index, guidance_index=guidance_index, cotangent=cotangent)


def reference(attn, resid, frozen, adapter_down_weight, adapter_up_weight, timestep_gate, guidance_gate, timestep_index, guidance_index, cotangent):
    sample_count = TOKENS // IMAGE_TOKENS
    gate = (timestep_gate[timestep_index] + guidance_gate[guidance_index])[:, None, :]
    down_portion = adapter_down_weight.astype(jnp.bfloat16)
    up_portion = adapter_up_weight.astype(jnp.bfloat16)
    frozen_output = jnp.dot(attn, frozen, preferred_element_type=jnp.float32)
    reduced_rank_rows = jnp.dot(attn, down_portion, preferred_element_type=jnp.float32).astype(jnp.bfloat16)
    adapter_lifted = jnp.dot(reduced_rank_rows, up_portion, preferred_element_type=jnp.float32)
    branch_output = (frozen_output + adapter_lifted).reshape(sample_count, IMAGE_TOKENS, MODEL_WIDTH)
    updated = resid.astype(jnp.float32).reshape(sample_count, IMAGE_TOKENS, MODEL_WIDTH) + gate * branch_output
    updated = updated.reshape(TOKENS, MODEL_WIDTH).astype(jnp.bfloat16)
    grad_out = (gate * cotangent.astype(jnp.float32).reshape(sample_count, IMAGE_TOKENS, MODEL_WIDTH)).reshape(TOKENS, MODEL_WIDTH).astype(jnp.bfloat16)
    grad_low = jnp.dot(grad_out, up_portion.T, preferred_element_type=jnp.float32).astype(jnp.bfloat16)
    grad_attn = jnp.dot(grad_out, frozen.T, preferred_element_type=jnp.float32) + jnp.dot(grad_low, down_portion.T, preferred_element_type=jnp.float32)
    grad_attn = grad_attn.astype(jnp.bfloat16)
    grad_scale = TOKENS ** -0.5
    grad_down = grad_scale * jnp.dot(attn.T, grad_low, preferred_element_type=jnp.float32)
    grad_up_t = grad_scale * jnp.dot(grad_out.T, reduced_rank_rows, preferred_element_type=jnp.float32)
    return updated, grad_attn, grad_down, grad_up_t
```

```python
import functools

import jax
import jax.numpy as jnp
from jax import lax
from jax.experimental import pallas as pl
from jax.experimental.pallas import tpu as pltpu
from jax.sharding import PartitionSpec as P

IMAGE_TOKENS = 4096
F32 = jnp.float32
BF16 = jnp.bfloat16


def contract_rows(left, right):
    return lax.dot_general(left, right, (((0,), (0,)), ((), ())), preferred_element_type=F32)


def contract_cols(left, right):
    return lax.dot_general(left, right, (((1,), (1,)), ((), ())), preferred_element_type=F32)


def matmul(left, right):
    return jnp.dot(left, right, preferred_element_type=F32)


def ring_order(chips):
    return [0] + list(range(1, chips, 2)) + list(range(chips - 2, 0, -2))


def ring_pairs(chips):
    order = ring_order(chips)
    pairs = []
    for place, chip in enumerate(order):
        after, before = order[(place + 1) % chips], order[(place - 1) % chips]
        pairs += [(2 * chip, 2 * after), (2 * chip + 1, 2 * before + 1)]
    return pairs


def step_kernel(spec, *refs):
    refs = list(refs)
    place = refs.pop(0)
    attn, gout, low, up, glow, down = refs[:6]
    refs = refs[6:]
    piece_refs = [refs.pop(0) for _ in spec["pieces"]]
    total_in = refs.pop(0) if spec["total_in"] else None
    part_in = refs.pop(0) if spec["part_in"] else None
    resid, gate = (refs.pop(0), refs.pop(0)) if spec["final"] else (None, None)
    for _ in range(spec["aliased"]):
        refs.pop(0)
    main_out = refs.pop(0)
    back_out = refs.pop(0)
    attn_v, gout_v, pieces_v, total_v, resid_v, result_v, back_v, load, store = refs
    rows = gout_v.shape[0]
    chips, span = spec["chips"], spec["span"]

    def cols(start, width):
        return pl.ds(pl.multiple_of(start, 128), width)

    def chip_cols(c):
        return cols(place[c], span)

    def block_cols(b):
        return cols(place[chips + b], spec["blocks"][b])

    loads = []

    def fetch(src, dst):
        copy = pltpu.make_async_copy(src, dst, load.at[len(loads)])
        copy.start()
        loads.append(copy)
        return copy

    get_attn = [fetch(attn.at[:, chip_cols(c)], attn_v.at[c]) for c in range(chips)]
    get_piece, get_total, get_gout, get_resid = [], [], [], []
    by_block = {}
    for i, (c, b) in enumerate(spec["pieces"]):
        by_block.setdefault(b, []).append((i, c))
    offset = []
    at = 0
    for b, width in enumerate(spec["blocks"]):
        offset.append(at)
        at += width
    get_piece = {}
    for b in by_block:
        width = spec["blocks"][b]
        for i, c in by_block[b]:
            get_piece[i] = fetch(piece_refs[i], pieces_v.at[i, :, pl.ds(0, width)])
        here = pl.ds(offset[b], width)
        get_gout.append(fetch(gout.at[:, block_cols(b)], gout_v.at[:, here]))
        if spec["total_in"]:
            get_total.append(fetch(total_in.at[:, block_cols(b)], total_v.at[:, here]))
        if spec["final"]:
            get_resid.append(fetch(resid.at[:, block_cols(b)], resid_v.at[:, here]))
    for copy in get_attn:
        copy.wait()
    stores = []
    back = [None] * chips
    for n, b in enumerate(by_block):
        width = spec["blocks"][b]
        here = pl.ds(offset[b], width)
        value = None
        for i, c in by_block[b]:
            get_piece[i].wait()
            term = matmul(attn_v[c], pieces_v[i, :, pl.ds(0, width)])
            value = term if value is None else value + term
        if spec["total_in"]:
            get_total[n].wait()
            value = value + total_v[:, here]
        else:
            value = value + matmul(low[...], up[:, block_cols(b)])
        if spec["final"]:
            get_resid[n].wait()
            value = resid_v[:, here].astype(F32) + gate[:, block_cols(b)] * value
        result_v[:, here] = value.astype(result_v.dtype)
        copy = pltpu.make_async_copy(result_v.at[:, here], main_out.at[:, block_cols(b)], store.at[len(stores)])
        copy.start()
        stores.append(copy)
        get_gout[n].wait()
        for i, c in by_block[b]:
            term = contract_cols(gout_v[:, here], pieces_v[i, :, pl.ds(0, width)])
            back[c] = term if back[c] is None else back[c] + term
    for c in range(chips):
        if spec["part_in"]:
            value = back[c] + part_in[...]
        else:
            value = back[c] + matmul(glow[...], down[:, chip_cols(c)])
        if spec["part_out"]:
            back_out[...] = value
        else:
            back_v[c] = value.astype(BF16)
            copy = pltpu.make_async_copy(back_v.at[c], back_out.at[:, chip_cols(c)], store.at[len(stores)])
            copy.start()
            stores.append(copy)
    for copy in stores:
        copy.wait()


def step(place, common, pieces, blocks, chips, span, total=None, part=None, part_out=False, final=None, main=None, back=None):
    rows, features = common[0].shape
    spec = dict(
        pieces=[(c, b) for _, c, b in pieces],
        blocks=blocks,
        chips=chips,
        span=span,
        total_in=total is not None,
        part_in=part is not None,
        part_out=part_out,
        final=final is not None,
    )
    vmem = pl.BlockSpec(memory_space=pltpu.VMEM)
    anywhere = pl.BlockSpec(memory_space=pl.ANY)
    args = [place, *common, *[p for p, _, _ in pieces]]
    specs = [pl.BlockSpec(memory_space=pltpu.SMEM), anywhere, anywhere, vmem, vmem, vmem, vmem]
    specs += [anywhere] * len(pieces)
    aliases = {}
    if total is not None:
        if final is None:
            aliases[len(args)] = 0
        args.append(total)
        specs.append(anywhere)
    if part is not None:
        args.append(part)
        specs.append(vmem)
    if final is not None:
        args += list(final)
        specs += [anywhere, vmem]
    aliased = 0
    if main is not None:
        aliases[len(args)] = 0
        args.append(main)
        specs.append(anywhere)
        aliased += 1
    if back is not None:
        aliases[len(args)] = 1
        args.append(back)
        specs.append(anywhere)
        aliased += 1
    spec["aliased"] = aliased
    main_type = BF16 if final is not None else F32
    width = sum(blocks)
    back_shape = jax.ShapeDtypeStruct((rows, span), F32) if part_out else jax.ShapeDtypeStruct((rows, features), BF16)
    n_load = chips + len(pieces) + 3 * len(blocks)
    n_store = len(blocks) + chips
    return pl.pallas_call(
        functools.partial(step_kernel, spec),
        out_shape=(jax.ShapeDtypeStruct((rows, features), main_type), back_shape),
        in_specs=specs,
        out_specs=(anywhere, vmem if part_out else anywhere),
        scratch_shapes=[
            pltpu.VMEM((chips, rows, span), BF16),
            pltpu.VMEM((rows, width), BF16),
            pltpu.VMEM((len(pieces), span, max(blocks)), BF16),
            pltpu.VMEM((rows, width) if total is not None else (8, 128), F32),
            pltpu.VMEM((rows, width) if final is not None else (16, 128), BF16),
            pltpu.VMEM((rows, width), main_type),
            pltpu.VMEM((chips, rows, span), BF16),
            pltpu.SemaphoreType.DMA((n_load,)),
            pltpu.SemaphoreType.DMA((n_store,)),
        ],
        input_output_aliases=aliases,
        compiler_params=pltpu.CompilerParams(vmem_limit_bytes=28 * 1024 * 1024),
        cost_estimate=pl.CostEstimate(
            flops=4 * rows * span * sum(blocks[b] for _, _, b in pieces),
            bytes_accessed=12 * 1024 * 1024,
            transcendentals=0,
        ),
    )(*args)


def scatter_sum(terms, axis_size):
    me = lax.axis_index("blk")
    bit = 1
    while bit < axis_size:
        pairs = [(i, i ^ bit) for i in range(axis_size)]
        mine = lax.rem(lax.div(me, bit), 2)
        slots = terms.reshape((terms.shape[0] // 2, 2) + terms.shape[1:])
        keep = jnp.where(mine == 0, slots[:, 0], slots[:, 1])
        give = jnp.where(mine == 0, slots[:, 1], slots[:, 0]).astype(BF16)
        terms = keep + lax.ppermute(give, "blk", pairs).astype(F32)
        bit *= 2
    return terms[0]


def ring_body(
    attn,
    resid,
    frozen,
    adapter_down_weight,
    adapter_up_weight,
    timestep_gate,
    guidance_gate,
    timestep_index,
    guidance_index,
    cotangent,
):
    rows, features = attn.shape
    axis_size = lax.axis_size("blk")
    chips = axis_size // 2
    shard = frozen.shape[0]
    span = 2 * shard
    third = features // 3
    half = third // 2
    me = lax.axis_index("blk")
    g = lax.axis_index("groups")
    chip, k = me // 2, me % 2
    core_pairs = [(i, i ^ 1) for i in range(axis_size)]
    ring = functools.partial(lax.ppermute, axis_name="blk", perm=ring_pairs(chips))
    swap = functools.partial(lax.ppermute, axis_name="blk", perm=core_pairs)
    cross = functools.partial(lax.ppermute, axis_name="groups", perm=[(0, 1), (1, 0)])
    order = jnp.asarray(ring_order(chips), jnp.int32)
    at = jnp.argmax(order == chip).astype(jnp.int32)

    def first_col(distance):
        return order[(at + distance + chips) % chips] * span

    own, common_third, others = g * 2 * third, third, (1 - g) * 2 * third

    def both_cores(start):
        mine = lax.dynamic_slice_in_dim(frozen, start, third, 1)
        other = swap(mine)
        low_rows, high_rows = jnp.where(k == 0, mine, other), jnp.where(k == 0, other, mine)
        return jnp.concatenate([low_rows, high_rows], 0)

    own_r, own_q = both_cores(own), both_cores(common_third)

    steps = chips // 2 - 1
    r, q = own_r, own_q
    r_all, q_all, x_all = [], [], []
    for _ in range(steps):
        r, q = ring(r), ring(q)
        x = cross(r)
        r_all.append(r)
        q_all.append(q)
        x_all.append(x)
    r_last = ring(lax.dynamic_slice_in_dim(r, k * half, half, 1))
    q_last = ring(lax.dynamic_slice_in_dim(q, k * half, half, 1))
    x_last = cross(r_last)

    own_x = both_cores(others)

    sample = me * rows // IMAGE_TOKENS
    t_row = lax.dynamic_index_in_dim(timestep_index, sample, 0, False)
    g_row = lax.dynamic_index_in_dim(guidance_index, sample, 0, False)
    gate = lax.dynamic_slice_in_dim(timestep_gate, t_row, 1, 0) + lax.dynamic_slice_in_dim(guidance_gate, g_row, 1, 0)
    down_half = adapter_down_weight.astype(BF16)
    up_half = adapter_up_weight.astype(BF16)
    low = matmul(attn, down_half).astype(BF16)
    gout = (gate * cotangent.astype(F32)).astype(BF16)
    glow = contract_cols(gout, up_half).astype(BF16)
    terms = jnp.concatenate([contract_rows(attn, glow), contract_rows(gout, low)], 1)
    summed = scatter_sum(terms.reshape(axis_size, shard, terms.shape[1]), axis_size)
    grad_scale = float(rows * axis_size) ** (-0.5)
    rank = glow.shape[1]
    grad_down, grad_up_t = grad_scale * summed[:, :rank], grad_scale * summed[:, rank:]

    common = (attn, gout, low, up_half, glow, down_half.T)
    blocks = [third] * 3

    def where(*values):
        return jnp.stack([jnp.asarray(v, jnp.int32) for v in values])

    total, grad_attn = step(
        where(first_col(0), own, common_third, others),
        common,
        [(own_r, 0, 0), (own_q, 0, 1), (own_x, 0, 2)],
        blocks, 1, span,
    )
    toward = 2 * k - 1
    for n in range(steps):
        pieces = [(r_all[n], 0, 0), (swap(r_all[n]), 1, 0)]
        pieces += [(q_all[n], 0, 1), (swap(q_all[n]), 1, 1)]
        pieces += [(x_all[n], 0, 2), (swap(x_all[n]), 1, 2)]
        total, grad_attn = step(
            where(first_col(toward * (n + 1)), first_col(-toward * (n + 1)), own, common_third, others),
            common, pieces, blocks, 2, span, total=total, back=grad_attn,
        )
    far = first_col(chips // 2)
    mine, theirs = k * half, (1 - k) * half
    updated, part = step(
        where(far, own + mine, own + theirs, common_third + mine, common_third + theirs),
        common,
        [(r_last, 0, 0), (swap(r_last), 0, 1), (q_last, 0, 2), (swap(q_last), 0, 3)],
        [half] * 4, 1, span, total=total, part_out=True, final=(resid, gate),
    )
    updated, grad_attn = step(
        where(far, others + mine, others + theirs),
        common,
        [(x_last, 0, 0), (swap(x_last), 0, 1)],
        [half] * 2, 1, span, total=total, part=part, final=(resid, gate), main=updated, back=grad_attn,
    )
    return updated, grad_attn, grad_down, grad_up_t


def gather_body(
    attn,
    resid,
    frozen,
    adapter_down_weight,
    adapter_up_weight,
    timestep_gate,
    guidance_gate,
    timestep_index,
    guidance_index,
    cotangent,
):
    rows, features = attn.shape
    axis_size = lax.axis_size("blk")
    whole = lax.all_gather(frozen, "blk", axis=0, tiled=True)
    sample = (lax.axis_index("blk") * rows + jnp.arange(rows, dtype=jnp.int32)) // IMAGE_TOKENS
    gate = timestep_gate[timestep_index[sample]] + guidance_gate[guidance_index[sample]]
    down_half = adapter_down_weight.astype(BF16)
    up_half = adapter_up_weight.astype(BF16)
    low = matmul(attn, down_half).astype(BF16)
    gout = (gate * cotangent.astype(F32)).astype(BF16)
    glow = contract_cols(gout, up_half).astype(BF16)
    terms = jnp.concatenate([contract_rows(attn, glow), contract_rows(gout, low)], 1)
    summed = lax.psum_scatter(terms, "blk", scatter_dimension=0, tiled=True)
    grad_scale = float(rows * axis_size) ** (-0.5)
    rank = glow.shape[1]
    base = matmul(attn, whole) + matmul(low, up_half)
    updated = (resid.astype(F32) + gate * base).astype(BF16)
    grad_attn = (contract_cols(gout, whole) + contract_cols(glow, down_half)).astype(BF16)
    return updated, grad_attn, grad_scale * summed[:, :rank], grad_scale * summed[:, rank:]


def solution(mesh):
    def run(attn, resid, frozen, *rest):
        axis_size, groups = mesh.shape["blk"], mesh.shape["groups"]
        rows, span = attn.shape[0] // (axis_size * groups), 2 * frozen.shape[0] // axis_size
        by_ring = groups == 2 and axis_size % 4 == 0 and axis_size >= 8 and axis_size & (axis_size - 1) == 0
        by_ring = by_ring and span % 128 == 0 and frozen.shape[1] % 768 == 0 and IMAGE_TOKENS % rows == 0
        spec = P(("groups", "blk"), None)
        return jax.shard_map(
            ring_body if by_ring else gather_body,
            mesh=mesh,
            in_specs=(spec, spec, P("blk", None), P(), P(), P(), P(), P("groups"), P("groups"), spec),
            out_specs=(spec, spec, spec, spec),
            check_vma=False,
        )(attn, resid, frozen, *rest)

    return run
```

```python
import functools

import jax
import jax.numpy as jnp
import numpy as np
from jax import lax
from jax.experimental import pallas as pl
from jax.experimental.pallas import tpu as pltpu
from jax.sharding import PartitionSpec as P

IMAGE_TOKENS = 4096
F32 = jnp.float32
BF16 = jnp.bfloat16


def contract_rows(left, right):
    return lax.dot_general(left, right, (((0,), (0,)), ((), ())), preferred_element_type=F32)


def contract_cols(left, right):
    return lax.dot_general(left, right, (((1,), (1,)), ((), ())), preferred_element_type=F32)


def matmul(left, right):
    return jnp.dot(left, right, preferred_element_type=F32)


def ring_order(chips):
    return [0] + list(range(1, chips, 2)) + list(range(chips - 2, 0, -2))


def ring_pairs(chips):
    order = ring_order(chips)
    pairs = []
    for place, chip in enumerate(order):
        after, before = order[(place + 1) % chips], order[(place - 1) % chips]
        pairs += [(2 * chip, 2 * after), (2 * chip + 1, 2 * before + 1)]
    return pairs


WIDTHS = (7, 4, 6, 7)
OWN = 6


def near(distance):
    return 5 + 2 * distance


def across(distance):
    return 6 + 2 * distance


def blocks_of(features):
    lane = features // 24
    return tuple(width * lane for width in WIDTHS)


def place_table(groups, axis_size, rows, span, features):
    chips = axis_size // 2
    order = ring_order(chips)
    wide, middle, third, _ = blocks_of(features)
    table = []
    for g in range(groups):
        for b in range(axis_size):
            chip, core = divmod(b, 2)
            at, toward = order.index(chip), 2 * core - 1
            far_side = wide + middle + third
            own, others = (0, far_side) if g == 0 else (far_side, 0)
            line = [core, b * rows // IMAGE_TOKENS, own, wide, wide + middle, others, chip * span]
            for n in range(1, chips // 2):
                line += [order[(at + toward * n) % chips] * span, order[(at - toward * n) % chips] * span]
            table.append(line + [order[(at + chips // 2) % chips] * span])
    return np.asarray(table, np.int32)


STEP_LIMIT = 16
VMEM_SPEC = pl.BlockSpec(memory_space=pltpu.VMEM)
SMEM_SPEC = pl.BlockSpec(memory_space=pltpu.SMEM)
HBM_SPEC = pl.BlockSpec(memory_space=pltpu.HBM)


def cols(start, width):
    return pl.ds(pl.multiple_of(start, 128), width)


def half_rows(core, shard):
    return pl.ds(pl.multiple_of(core * shard, 16), shard)


def call(kernel, args, specs, out_shape, out_specs, scratch=(), aliases=None, weight=1, limit=16):
    return pl.pallas_call(
        kernel,
        in_specs=specs,
        out_shape=out_shape,
        out_specs=out_specs,
        scratch_shapes=scratch,
        input_output_aliases=aliases or {},
        compiler_params=pltpu.CompilerParams(vmem_limit_bytes=limit * 1024 * 1024),
        cost_estimate=pl.CostEstimate(flops=0, bytes_accessed=weight, transcendentals=0),
    )(*args)


def cut(place, frozen, blocks):
    shard = frozen.shape[0]

    def kernel(place, frozen, *refs):
        outs, sems = refs[:-1], refs[-1]
        copies = []
        for n, width in enumerate(blocks):
            copies.append(pltpu.make_async_copy(frozen.at[:, cols(place[2 + n], width)], outs[n], sems.at[n]))
            copies[n].start()
        for copy in copies:
            copy.wait()

    return call(
        kernel, (place, frozen), [SMEM_SPEC, HBM_SPEC], [jax.ShapeDtypeStruct((shard, w), BF16) for w in blocks],
        [VMEM_SPEC] * len(blocks), [pltpu.SemaphoreType.DMA((len(blocks),))], limit=4,
    )


def pair(place, mine, theirs, blocks, which):
    shard = theirs.shape[0]

    def kernel(place, *refs):
        theirs, refs = refs[len(which)], refs[: len(which)] + refs[len(which) + 1 :]
        for n, block in enumerate(which):
            out = refs[len(which) + n]
            out[half_rows(place[0], shard), :] = refs[n][...]
            out[half_rows(1 - place[0], shard), :] = theirs[:, cols(place[2 + block], blocks[block])]

    return call(
        kernel, (place, *[mine[block] for block in which], theirs), [SMEM_SPEC] + [VMEM_SPEC] * (len(which) + 1),
        [jax.ShapeDtypeStruct((2 * shard, blocks[block]), BF16) for block in which], [VMEM_SPEC] * len(which), limit=4,
    )


def own_half(place, whole):
    shard, width = whole.shape[0] // 2, whole.shape[1]

    def kernel(place, whole, out):
        out[...] = whole[half_rows(place[0], shard), :]

    return call(
        kernel, (place, whole), [SMEM_SPEC, VMEM_SPEC], jax.ShapeDtypeStruct((shard, width), BF16), VMEM_SPEC, limit=4,
    )


def adapter(place, t_index, g_index, attn, cotangent, down_t, up, t_gate, g_gate, blocks, chips):
    rows, features = attn.shape
    rank = up.shape[0]
    span = features // chips

    def kernel(place, t_index, g_index, attn, cotangent, down_t, up, t_gate, g_gate,
               gate_out, gout_out, low_out, up_out, down_out, terms_out, give_out, gout_v):
        sample = place[1]
        gate = t_gate[pl.ds(t_index[sample], 1), :] + g_gate[pl.ds(g_index[sample], 1), :]
        gout = (gate * cotangent[...].astype(F32)).astype(BF16)
        gout_v[...] = gout
        up_half = up[...].astype(BF16)
        down_half = down_t[...].astype(BF16)
        down_out[...] = down_half
        low = contract_cols(attn[...], down_half).astype(BF16)
        glow = contract_cols(gout, up_half).astype(BF16)
        low_out[...] = low
        at = 0
        for n, width in enumerate(blocks):
            here, there = pl.ds(at, width), cols(place[2 + n], width)
            gout_out[:, here] = gout_v[:, there]
            up_out[:, here] = up[:, there].astype(BF16)
            gate_out[:, here] = t_gate[pl.ds(t_index[sample], 1), there] + g_gate[pl.ds(g_index[sample], 1), there]
            at += width
        gout_out[:, pl.ds(features, 128)] = jnp.concatenate([glow, jnp.zeros((rows, 128 - rank), BF16)], 1)
        both = jnp.concatenate([contract_rows(glow, attn[...]), contract_rows(low, gout)], 0)
        terms = both.T.reshape(chips, span, 2 * rank)
        terms_out[...] = terms
        give_out[...] = terms.astype(BF16)

    shape = jax.ShapeDtypeStruct
    return call(
        kernel,
        (place, t_index, g_index, attn, cotangent, down_t, up, t_gate, g_gate),
        [SMEM_SPEC] * 3 + [VMEM_SPEC] * 6,
        [
            shape((1, features), F32),
            shape((rows, features + 128), BF16),
            shape((rows, rank), BF16),
            shape((rank, features), BF16),
            shape((rank, features), BF16),
            shape((chips, span, 2 * rank), F32),
            shape((chips, span, 2 * rank), BF16),
        ],
        [VMEM_SPEC] * 7,
        [pltpu.VMEM((rows, features), BF16)],
    )


def chunk(place, slot, block, width, terms, theirs, which):
    _, span, lanes = terms.shape
    shard = span // 2

    def kernel(place, block, terms, theirs, out):
        chip, rest = lax.div(place[slot], span), pl.ds(width, lanes)
        mine, other = half_rows(place[0], shard), half_rows(1 - place[0], shard)
        out[:, pl.ds(0, width)] = block[:, pl.ds(0, width)]
        if which == "first":
            out[mine, rest] = (terms[chip, mine, :] + theirs[chip, mine, :].astype(F32)).astype(BF16)
            out[other, rest] = jnp.zeros((shard, lanes), BF16)
        else:
            value = terms[chip] + theirs[chip].astype(F32) + block[:, rest].astype(F32)
            out[:, rest] = value.astype(BF16)

    return call(
        kernel, (place, block, terms, theirs), [SMEM_SPEC] + [VMEM_SPEC] * 3,
        jax.ShapeDtypeStruct((span, width + lanes), BF16), VMEM_SPEC, limit=8,
    )


def last_chunk(place, slot, block, second, width, terms, theirs):
    _, span, lanes = terms.shape
    shard, more = span // 2, second.shape[1]

    def kernel(place, block, second, terms, theirs, out):
        chip = lax.div(place[slot], span)
        mine, rest = half_rows(place[0], shard), pl.ds(width, lanes)
        value = (block[:, rest].astype(F32) + terms[chip] + theirs[chip].astype(F32)).astype(BF16)
        out[:, pl.ds(0, width)] = block[mine, pl.ds(0, width)]
        out[:, pl.ds(width, more)] = second[mine, :]
        out[:, pl.ds(width + more, lanes)] = value[:shard]
        out[:, pl.ds(width + more + lanes, lanes)] = value[shard:]

    return call(
        kernel, (place, block, second, terms, theirs), [SMEM_SPEC] + [VMEM_SPEC] * 4,
        jax.ShapeDtypeStruct((shard, width + more + 2 * lanes), BF16), VMEM_SPEC, limit=8,
    )


def finish(place, slot, terms, theirs, block, block_theirs, width, scale):
    _, span, lanes = terms.shape
    shard = span // 2

    def kernel(place, terms, theirs, block, block_theirs, first, second):
        chip = lax.div(place[slot], span)
        mine, rest = half_rows(place[0], shard), cols(width + place[0] * lanes, lanes)
        value = terms[chip, mine, :] + theirs[chip, mine, :].astype(F32)
        value = value + block[:, rest].astype(F32) + block_theirs[:, rest].astype(F32)
        value = (scale * value).T
        first[...] = value[: lanes // 2]
        second[...] = value[lanes // 2 :]

    shape = jax.ShapeDtypeStruct((lanes // 2, shard), F32)
    args = (place, terms, theirs, block, block_theirs)
    return call(kernel, args, [SMEM_SPEC] + [VMEM_SPEC] * (len(args) - 1), [shape] * 2, [VMEM_SPEC] * 2, limit=8)


def side_step(place, distance, attn, gout, mates, down_t, rank, blocks, ring_blocks, x_block, totals, parts, grad_attn, gives, last):
    rows, features = attn.shape
    span = ring_blocks[0].shape[0]
    starts = [sum(blocks[:n]) for n in range(len(blocks))]
    names, args, specs, aliases = [], [], [], {}
    outs, out_specs = [], []

    def give(name, array, spec=VMEM_SPEC):
        names.append(name)
        args.append(array)
        specs.append(spec)

    def produce(name, shape, dtype, spec=VMEM_SPEC, old=None):
        if old is not None:
            aliases[len(args)] = len(outs)
            give(name + "_in", old, spec)
        outs.append((name, jax.ShapeDtypeStruct(shape, dtype)))
        out_specs.append(spec)

    give("place", place, SMEM_SPEC)
    give("attn", attn)
    give("gout", gout)
    give("attn_t", mates[0])
    give("gout_t", mates[1])
    give("down", down_t)
    for n, array in enumerate(ring_blocks):
        give(("ring", n), array)
    if x_block is not None:
        give("x", x_block)
        give("part_old", parts[0])
        give("part_t_old", parts[1])
    if last:
        for n, array in enumerate(gives):
            give(("given", n), array)
    produce("total", (rows, features), F32, old=totals[0])
    if last:
        give("total_t_in", totals[1])
        produce("send", (rows, features + (len(gives) + 2) * span), BF16)
    else:
        produce("total_t", (rows, features), F32, old=totals[1])
    produce("part", (rows, span), F32)
    if not last:
        produce("part_t", (rows, span), F32)
    if x_block is not None:
        produce("grad", (rows, features), BF16, HBM_SPEC, grad_attn)
    if x_block is not None and not last:
        produce("give", (rows, span), BF16)
    out_names = [name for name, _ in outs]

    def kernel(*refs):
        ref = dict(zip(names + [("out", name) for name in out_names], refs))
        grad_v, store = refs[len(names) + len(out_names) :]
        place = ref["place"]
        stores = []

        def put(src, dst):
            copy = pltpu.make_async_copy(src, dst, store.at[len(stores)])
            copy.start()
            stores.append(copy)

        def both(name, at):
            return jnp.concatenate([ref[name][:, at], ref[name + "_t"][:, at]], 0)

        def set_total_t(at, value):
            if last:
                ref[("out", "send")][:, at] = value.astype(BF16)
            else:
                ref[("out", "total_t")][:, at] = value

        if x_block is not None:
            at, there = cols(place[near(distance - 1)], span), pl.ds(starts[3], blocks[3])
            value = matmul(both("attn", at), ref["x"][...])
            ref[("out", "total")][:, there] = ref["total_in"][:, there] + value[:rows]
            value_t = value[rows:]
            if distance > 2:
                value_t = value_t + ref["total_t_in"][:, there]
            set_total_t(there, value_t)
            value = contract_cols(both("gout", there), ref["x"][...])
            grad_v[...] = (value[:rows] + ref["part_old"][...]).astype(BF16)
            put(grad_v, ref[("out", "grad")].at[:, at])
            value = (value[rows:] + ref["part_t_old"][...]).astype(BF16)
            if last:
                for n in range(len(gives)):
                    ref[("out", "send")][:, pl.ds(features + n * span, span)] = ref[("given", n)][...]
                ref[("out", "send")][:, pl.ds(features + len(gives) * span, span)] = value
            else:
                ref[("out", "give")][...] = value
        at = cols(place[near(distance)], span)
        glow = both("gout", pl.ds(features, rank))
        back = matmul(glow, ref["down"][:, at])
        a = both("attn", at)
        for n in range(3):
            there, width = pl.ds(starts[n], blocks[n]), blocks[n]
            piece = ref[("ring", n)][:, pl.ds(0, width)]
            value = matmul(a, piece)
            ref[("out", "total")][:, there] = ref["total_in"][:, there] + value[:rows]
            value_t = value[rows:]
            if distance > 1:
                value_t = value_t + ref["total_t_in"][:, there]
            set_total_t(there, value_t)
            back = back + contract_cols(both("gout", there), piece)
        ref[("out", "part")][...] = back[:rows]
        if last:
            ref[("out", "send")][:, pl.ds(features + (len(gives) + 1) * span, span)] = back[rows:].astype(BF16)
        else:
            ref[("out", "part_t")][...] = back[rows:]
        for copy in stores:
            copy.wait()

    result = call(
        kernel, args, specs, [shape for _, shape in outs], out_specs,
        [pltpu.VMEM((rows, span), BF16), pltpu.SemaphoreType.DMA((2,))], aliases, limit=STEP_LIMIT,
    )
    result = dict(zip(out_names, result))
    return (
        (result["total"], result.get("total_t")), (result["part"], result.get("part_t")), result.get("grad", grad_attn),
        result["send"] if last else result.get("give"),
    )


def step(place, jobs, attn, blocks, grads, total=None, add=None, final=None, updated=None, grad_attn=None, extra=None):
    rows, features = attn.shape
    gout, down_t, rank = grads
    place_span = span_of(jobs)
    starts = [sum(blocks[:n]) for n in range(len(blocks))]
    names, args, specs, aliases = [], [], [], {}

    def give(name, array, spec=VMEM_SPEC):
        names.append(name)
        args.append(array)
        specs.append(spec)

    give("place", place, SMEM_SPEC)
    give("attn", attn)
    give("gout", gout)
    if any(job["part"] is None for job in jobs):
        give("down", down_t)
    if extra is not None:
        give("extra", extra[0])
    if add is not None:
        give("low", add[0])
        give("up", add[1])
    if any(job["final"] for job in jobs):
        give("resid", final[0], HBM_SPEC)
        give("gate", final[1])
    outs, out_specs = [], []

    def produce(name, shape, dtype, spec, old=None):
        if old is not None:
            aliases[len(args)] = len(outs)
            give(name + "_in", old, spec)
        outs.append((name, jax.ShapeDtypeStruct(shape, dtype)))
        out_specs.append(spec)

    if not all(job["final"] for job in jobs):
        produce("total", (rows, features), F32, VMEM_SPEC, total)
    elif total is not None:
        give("total_in", total)
    if any(job["final"] for job in jobs):
        produce("updated", (rows, features), BF16, HBM_SPEC, updated)
    if not all(job["open"] for job in jobs):
        produce("grad", (rows, features), BF16, HBM_SPEC, grad_attn)
    scratch = []
    tiny = pltpu.VMEM((16, 128), BF16)
    for j, job in enumerate(jobs):
        some = job["pieces"][0][0]
        job["halves"] = halves = isinstance(some, tuple)
        job["span"] = span = place_span
        job["width"] = width = sum(blocks[n] for n in job["blocks"])
        job["deep"] = deep = span * len(job["chips"])
        for n, per in enumerate(job["pieces"]):
            for c, array in enumerate(per):
                for h, half in enumerate(array if halves else (array,)):
                    give(("piece", j, n, c, h), half.array if isinstance(half, Part) else half)
        if job["part"] is not None:
            for c, array in enumerate(job["part"]):
                if array is not None:
                    give(("part", j, c), array)
        if job["open"]:
            produce(("open", j), (rows, deep), F32, VMEM_SPEC)
        scratch += [
            pltpu.VMEM((deep, width), BF16) if halves else tiny,
            pltpu.VMEM((rows, width), BF16) if job["final"] else tiny,
            pltpu.VMEM((rows, width), BF16) if job["final"] else tiny,
            tiny if job["open"] else pltpu.VMEM((rows, deep), BF16),
        ]
    n_job = len(scratch)
    scratch += [pltpu.SemaphoreType.DMA((8,)), pltpu.SemaphoreType.DMA((8,))]
    out_names = [name for name, _ in outs]

    def kernel(*refs):
        ref = dict(zip(names + [("out", name) for name in out_names], refs))
        rest = refs[len(names) + len(out_names) :]
        load, store = rest[n_job:]
        place = ref["place"]
        loads, stores = {}, []

        def put(src, dst):
            copy = pltpu.make_async_copy(src, dst, store.at[len(stores)])
            copy.start()
            stores.append(copy)

        for j, job in enumerate(jobs):
            if job["final"]:
                for block in job["blocks"]:
                    here = pl.ds(starts[block] - starts[job["blocks"][0]], blocks[block])
                    src = ref["resid"].at[:, cols(place[2 + block], blocks[block])]
                    loads[j, block] = pltpu.make_async_copy(src, rest[4 * j + 1].at[:, here], load.at[len(loads)])
                    loads[j, block].start()
        if extra is not None and extra[1] is not None:
            span = jobs[0]["span"]
            for n, slot in enumerate(extra[1]):
                put(ref["extra"].at[:, pl.ds(features + n * span, span)], ref[("out", "grad")].at[:, cols(place[slot], span)])
        for j, job in enumerate(jobs):
            frozen_v, resid_v, result_v, back_v = rest[4 * j : 4 * j + 4]
            span = job["span"]
            chip_cols = [cols(place[s], span) for s in job["chips"]]
            back = [None] * len(chip_cols)
            for n, block in enumerate(job["blocks"]):
                width = blocks[block]
                here, there = pl.ds(starts[block] - starts[job["blocks"][0]], width), pl.ds(starts[block], width)
                value = ref["total_in"][:, there] if total is not None else matmul(ref["low"][...], ref["up"][:, there])
                if extra is not None:
                    value = value + ref["extra"][:, there].astype(F32)
                for c, at in enumerate(chip_cols):
                    if job["halves"]:
                        shard = span // 2
                        for h, core in enumerate((place[0], 1 - place[0])):
                            to = pl.ds(pl.multiple_of(c * span + core * shard, 16), shard)
                            half = job["pieces"][n][c][h]
                            row, col = (half.row, half.col) if isinstance(half, Part) else (0, 0)
                            frozen_v[to, here] = ref[("piece", j, n, c, h)][pl.ds(row, shard), pl.ds(col, width)]
                        piece = frozen_v[pl.ds(c * span, span), here]
                    else:
                        piece = ref[("piece", j, n, c, 0)][pl.ds(0, span), :]
                    value = value + matmul(ref["attn"][:, at], piece)
                    term = contract_cols(ref["gout"][:, there], piece)
                    back[c] = term if back[c] is None else back[c] + term
                if job["final"]:
                    loads[j, block].wait()
                    result_v[:, here] = (resid_v[:, here].astype(F32) + ref["gate"][:, there] * value).astype(BF16)
                    put(result_v.at[:, here], ref[("out", "updated")].at[:, cols(place[2 + block], width)])
                else:
                    ref[("out", "total")][:, there] = value
            for c, at in enumerate(chip_cols):
                mine = pl.ds(c * span, span)
                if job["part"] is None:
                    value = back[c] + matmul(ref["gout"][:, pl.ds(features, rank)], ref["down"][:, at])
                else:
                    from_mate = job["part"][c] is None
                    part = ref["extra"][:, pl.ds(features + len(extra[1]) * span, span)].astype(F32) if from_mate else ref[("part", j, c)][...]
                    value = back[c] + part
                if job["open"]:
                    ref[("out", ("open", j))][:, mine] = value
                else:
                    back_v[:, mine] = value.astype(BF16)
                    put(back_v.at[:, mine], ref[("out", "grad")].at[:, at])
        for copy in stores:
            copy.wait()

    result = call(
        kernel, args, specs, [shape for _, shape in outs], out_specs, scratch, aliases,
        weight=12, limit=STEP_LIMIT,
    )
    result = dict(zip(out_names, result))
    opened = [result[("open", j)] for j, job in enumerate(jobs) if job["open"]]
    return result.get("total", total), result.get("updated", updated), result.get("grad", grad_attn), *opened


class Part:
    def __init__(self, array, row=0, col=0):
        self.array, self.row, self.col = array, row, col


def span_of(jobs):
    sizes = []
    for job in jobs:
        some = job["pieces"][0][0]
        sizes.append(2 * some[0].shape[0] if isinstance(some, tuple) else some.shape[0])
    return min(sizes)


def job(chips, blocks, pieces, part=None, open=False, final=False):
    return dict(chips=chips, blocks=blocks, pieces=pieces, part=part, open=open, final=final)


EDGES = dict(
    gout="s",
    k0="s",
    r1="T",
    x1="T",
    q1="rTm",
    s2="Tx",
    k2="x",
    r3="S",
    x3="S",
    q3="Tx",
    s3="Tx",
    k3="x",
    r4="TX",
    x4="s",
    q4="rT",
    send="r",
    q5="e",
)
WHEN = "srs"


def after(value, *others):
    return lax.optimization_barrier((value, *others))[0]


def ring_body(
    table,
    attn,
    resid,
    frozen,
    adapter_down_weight,
    adapter_up_weight,
    timestep_gate,
    guidance_gate,
    timestep_index,
    guidance_index,
    cotangent,
):
    rows, features = attn.shape
    axis_size = lax.axis_size("blk")
    chips = axis_size // 2
    blocks = blocks_of(features)
    me = lax.axis_index("blk")
    device = lax.axis_index("groups") * axis_size + me
    core_pairs = [(i, i ^ 1) for i in range(axis_size)]
    ring = functools.partial(lax.ppermute, axis_name="blk", perm=ring_pairs(chips))
    swap = functools.partial(lax.ppermute, axis_name="blk", perm=core_pairs)
    cross = functools.partial(lax.ppermute, axis_name="groups", perm=[(0, 1), (1, 0)])
    place = lax.dynamic_index_in_dim(jnp.asarray(table), device, 0, False)

    rank = adapter_up_weight.shape[0]
    steps = chips // 2 - 1
    far = near(steps + 1)
    wide = blocks[1]
    def gate(name, value, **have):
        others = [have[k] for k in EDGES.get(name, "") if have.get(k) is not None]
        return after(value, *others) if others else value

    theirs = swap(frozen)
    own = pair(place, cut(place, frozen, blocks), theirs, blocks, [0, 1, 2, 3])
    r, q, s = [None, ring(own[0])], [None], [None, ring(own[2])]
    known = dict(o=own[0], p=own[1], r=r[1], s=s[1])
    attn_t = known["a"] = swap(gate("attn", attn, **known))
    gate_row, gout, low, up, down_t, terms, given = adapter(
        place, timestep_index, guidance_index, attn, gate("adapter", cotangent, **known),
        adapter_down_weight.T, adapter_up_weight, timestep_gate, guidance_gate, blocks, chips,
    )
    terms_t = known["t"] = swap(given)
    first_q = known["f"] = chunk(place, far, own[1], wide, terms, terms_t, "first")
    q.append(ring(first_q))
    known["q"] = q[1]
    gout_t = known["m"] = swap(gate("gout", gout, **known))
    grads = (gout, down_t, rank)
    total, _, grad_attn = step(
        place, [job([OWN], [0, 1, 2, 3], [[block] for block in own])], attn, blocks,
        (gate("k0", gout, **known), down_t, rank), add=(low, up),
    )
    totals, parts, give, gives, x = (total, None), None, None, [], [None]

    def run(n, arrival, **have):
        nonlocal totals, parts, grad_attn, give
        last = n == steps
        totals, parts, grad_attn, give = side_step(
            place, n, attn, gate(f"k{n}", after(gout, arrival), **have), (attn_t, gout_t), down_t, rank, blocks,
            [r[n], q[n], s[n]], x[n - 1], totals, parts, grad_attn, gives, last,
        )
        if give is not None and not last:
            gives.append(give)

    for n in range(1, steps + 1):
        last = n == steps
        prev = dict(T=totals[0], x=x[n - 1], S=s[n - 1], Q=q[n - 1])
        r[n] = gate(f"r{n}", r[n], **{**known, **prev})
        r.append(ring(own_half(place, r[n]) if last else r[n]))
        x.append(cross(gate(f"x{n}", r[n], **prev)))
        if n > 1 and WHEN[n - 2] == "r":
            run(n - 1, r[n], x=x[n - 1], X=x[n - 2])
        q[n] = gate(f"q{n}", q[n], **{**known, "r": r[n], "T": totals[0], "x": x[n - 1]})
        if not last:
            q.append(ring(chunk(place, across(steps + 1 - n), q[n], wide, terms, terms_t, "middle")))
        if n > 1 and WHEN[n - 2] == "q":
            run(n - 1, q[n], x=x[n - 1], X=x[n - 2])
        s[n] = gate(f"s{n}", s[n], **{**known, "q": q[n], "r": r[n], "T": totals[0], "x": x[n - 1]})
        if last:
            q.append(ring(last_chunk(place, across(1), q[n], s[n], wide, terms, terms_t)))
        else:
            s.append(ring(s[n]))
        if WHEN[n - 1] == "s":
            run(n, s[n], x=x[n - 1])

    r_far = gate("r4", r[steps + 1], X=x[steps], T=totals[0], s=s[steps], q=q[steps])
    x_far = cross(gate("x4", r_far, X=x[steps], T=totals[0], s=s[steps]))
    if WHEN[steps - 1] == "r":
        run(steps, r_far, X=x[steps])
    x_before = gate("back", x[steps], r=r_far)
    x_swapped, r_swapped = swap(x_before), swap(r_far)
    swaps = dict(v=x_swapped, w=r_swapped)
    q_far = gate("q4", q[steps + 1], r=r_far, T=totals[0], **swaps)
    if WHEN[steps - 1] == "q":
        run(steps, q_far, X=x[steps])
    extra = swap(gate("send", give, r=r_far, X=x[steps], q=q_far))
    q_swapped = swap(gate("q5", q_far, e=extra, **swaps))
    grad_scale = float(rows * axis_size) ** (-0.5)
    grad_down_t, grad_up = finish(place, OWN, terms, terms_t, q_far, q_swapped, wide + blocks[2], grad_scale)
    x_job = job([near(steps), across(steps)], [3], [[x_before, x_swapped]], part=[parts[0], None])
    s_piece = (Part(q_far, 0, wide), Part(q_swapped, 0, wide))
    far_job = job([far], [0, 1, 2], [[(r_far, r_swapped)], [(q_far, q_swapped)], [s_piece]], open=True, final=True)
    total, updated, grad_attn, part = step(
        place, [x_job, far_job], attn, blocks, (after(gout, grad_down_t), down_t, rank), total=totals[0],
        final=(resid, gate_row), grad_attn=grad_attn, extra=(extra, [across(n) for n in range(1, steps)]),
    )
    x_far = gate("x5", x_far, s=q_far, q=q_far, T=total)
    _, updated, grad_attn = step(
        place, [job([far], [3], [[(x_far, swap(x_far))]], part=[part], final=True)],
        attn, blocks, grads, total=total, final=(resid, gate_row), updated=updated, grad_attn=grad_attn,
    )
    return updated, grad_attn, grad_down_t.T, grad_up.T


def gather_body(
    attn,
    resid,
    frozen,
    adapter_down_weight,
    adapter_up_weight,
    timestep_gate,
    guidance_gate,
    timestep_index,
    guidance_index,
    cotangent,
):
    rows, features = attn.shape
    axis_size = lax.axis_size("blk")
    whole = lax.all_gather(frozen, "blk", axis=0, tiled=True)
    sample = (lax.axis_index("blk") * rows + jnp.arange(rows, dtype=jnp.int32)) // IMAGE_TOKENS
    gate = timestep_gate[timestep_index[sample]] + guidance_gate[guidance_index[sample]]
    down_half = adapter_down_weight.astype(BF16)
    up_half = adapter_up_weight.astype(BF16)
    low = matmul(attn, down_half).astype(BF16)
    gout = (gate * cotangent.astype(F32)).astype(BF16)
    glow = contract_cols(gout, up_half).astype(BF16)
    terms = jnp.concatenate([contract_rows(attn, glow), contract_rows(gout, low)], 1)
    summed = lax.psum_scatter(terms, "blk", scatter_dimension=0, tiled=True)
    grad_scale = float(rows * axis_size) ** (-0.5)
    rank = glow.shape[1]
    base = matmul(attn, whole) + matmul(low, up_half)
    updated = (resid.astype(F32) + gate * base).astype(BF16)
    grad_attn = (contract_cols(gout, whole) + contract_cols(glow, down_half)).astype(BF16)
    return updated, grad_attn, grad_scale * summed[:, :rank], grad_scale * summed[:, rank:]


def solution(mesh):
    def run(attn, resid, frozen, *rest):
        axis_size, groups = mesh.shape["blk"], mesh.shape["groups"]
        rows, span = attn.shape[0] // (axis_size * groups), 2 * frozen.shape[0] // axis_size
        by_ring = groups == 2 and axis_size == 16
        by_ring = by_ring and span % 128 == 0 and frozen.shape[1] % 3072 == 0 and IMAGE_TOKENS % rows == 0
        body = gather_body
        if by_ring:
            table = place_table(groups, axis_size, rows, span, frozen.shape[1])
            body = functools.partial(ring_body, table)
        spec = P(("groups", "blk"), None)
        return jax.shard_map(
            body,
            mesh=mesh,
            in_specs=(spec, spec, P("blk", None), P(), P(), P(), P(), P("groups"), P("groups"), spec),
            out_specs=(spec, spec, spec, spec),
            check_vma=False,
        )(attn, resid, frozen, *rest)

    return run
```

```python
import functools

import jax
import jax.numpy as jnp
import numpy as np
from jax import lax
from jax.experimental import pallas as pl
from jax.experimental.pallas import tpu as pltpu
from jax.sharding import PartitionSpec as P

IMAGE_TOKENS = 4096
F32 = jnp.float32
BF16 = jnp.bfloat16


def contract_rows(left, right):
    return lax.dot_general(left, right, (((0,), (0,)), ((), ())), preferred_element_type=F32)


def contract_cols(left, right):
    return lax.dot_general(left, right, (((1,), (1,)), ((), ())), preferred_element_type=F32)


def matmul(left, right):
    return jnp.dot(left, right, preferred_element_type=F32)


def ring_order(chips):
    return [0] + list(range(1, chips, 2)) + list(range(chips - 2, 0, -2))


def ring_pairs(chips):
    order = ring_order(chips)
    pairs = []
    for place, chip in enumerate(order):
        after, before = order[(place + 1) % chips], order[(place - 1) % chips]
        pairs += [(2 * chip, 2 * after), (2 * chip + 1, 2 * before + 1)]
    return pairs


WIDTHS = (7, 4, 6, 7)
OWN = 6


def near(distance):
    return 5 + 2 * distance


def across(distance):
    return 6 + 2 * distance


def blocks_of(features):
    lane = features // 24
    return tuple(width * lane for width in WIDTHS)


def place_table(groups, axis_size, rows, span, features):
    chips = axis_size // 2
    order = ring_order(chips)
    wide, middle, third, _ = blocks_of(features)
    table = []
    for g in range(groups):
        for b in range(axis_size):
            chip, core = divmod(b, 2)
            at, toward = order.index(chip), 2 * core - 1
            far_side = wide + middle + third
            own, others = (0, far_side) if g == 0 else (far_side, 0)
            line = [core, b * rows // IMAGE_TOKENS, own, wide, wide + middle, others, chip * span]
            for n in range(1, chips // 2):
                line += [order[(at + toward * n) % chips] * span, order[(at - toward * n) % chips] * span]
            table.append(line + [order[(at + chips // 2) % chips] * span])
    return np.asarray(table, np.int32)


STEP_LIMIT = 16
VMEM_SPEC = pl.BlockSpec(memory_space=pltpu.VMEM)
SMEM_SPEC = pl.BlockSpec(memory_space=pltpu.SMEM)
HBM_SPEC = pl.BlockSpec(memory_space=pltpu.HBM)


def cols(start, width):
    return pl.ds(pl.multiple_of(start, 128), width)


def half_rows(core, shard):
    return pl.ds(pl.multiple_of(core * shard, 16), shard)


def call(kernel, args, specs, out_shape, out_specs, scratch=(), aliases=None, weight=1, limit=16):
    return pl.pallas_call(
        kernel,
        in_specs=specs,
        out_shape=out_shape,
        out_specs=out_specs,
        scratch_shapes=scratch,
        input_output_aliases=aliases or {},
        compiler_params=pltpu.CompilerParams(vmem_limit_bytes=limit * 1024 * 1024),
        cost_estimate=pl.CostEstimate(flops=0, bytes_accessed=weight, transcendentals=0),
    )(*args)


def cut(place, frozen, blocks):
    shard = frozen.shape[0]

    def kernel(place, frozen, *refs):
        outs, sems = refs[:-1], refs[-1]
        copies = []
        for n, width in enumerate(blocks):
            copies.append(pltpu.make_async_copy(frozen.at[:, cols(place[2 + n], width)], outs[n], sems.at[n]))
            copies[n].start()
        for copy in copies:
            copy.wait()

    return call(
        kernel, (place, frozen), [SMEM_SPEC, HBM_SPEC], [jax.ShapeDtypeStruct((shard, w), BF16) for w in blocks],
        [VMEM_SPEC] * len(blocks), [pltpu.SemaphoreType.DMA((len(blocks),))], limit=4,
    )


def pair(place, mine, theirs, blocks, which):
    shard = theirs.shape[0]

    def kernel(place, *refs):
        theirs, refs = refs[len(which)], refs[: len(which)] + refs[len(which) + 1 :]
        for n, block in enumerate(which):
            out = refs[len(which) + n]
            out[half_rows(place[0], shard), :] = refs[n][...]
            out[half_rows(1 - place[0], shard), :] = theirs[:, cols(place[2 + block], blocks[block])]

    return call(
        kernel, (place, *[mine[block] for block in which], theirs), [SMEM_SPEC] + [VMEM_SPEC] * (len(which) + 1),
        [jax.ShapeDtypeStruct((2 * shard, blocks[block]), BF16) for block in which], [VMEM_SPEC] * len(which), limit=4,
    )


def own_half(place, whole):
    shard, width = whole.shape[0] // 2, whole.shape[1]

    def kernel(place, whole, out):
        out[...] = whole[half_rows(place[0], shard), :]

    return call(
        kernel, (place, whole), [SMEM_SPEC, VMEM_SPEC], jax.ShapeDtypeStruct((shard, width), BF16), VMEM_SPEC, limit=4,
    )


def adapter(place, t_index, g_index, attn, cotangent, down_t, up, t_gate, g_gate, blocks, chips):
    rows, features = attn.shape
    rank = up.shape[0]
    span = features // chips

    def kernel(place, t_index, g_index, attn, cotangent, down_t, up, t_gate, g_gate,
               gate_out, gout_out, low_out, up_out, down_out, terms_out, give_out, gout_v):
        sample = place[1]
        gate = t_gate[pl.ds(t_index[sample], 1), :] + g_gate[pl.ds(g_index[sample], 1), :]
        gout = (gate * cotangent[...].astype(F32)).astype(BF16)
        gout_v[...] = gout
        up_half = up[...].astype(BF16)
        down_half = down_t[...].astype(BF16)
        down_out[...] = down_half
        low = contract_cols(attn[...], down_half).astype(BF16)
        glow = contract_cols(gout, up_half).astype(BF16)
        low_out[...] = low
        at = 0
        for n, width in enumerate(blocks):
            here, there = pl.ds(at, width), cols(place[2 + n], width)
            gout_out[:, here] = gout_v[:, there]
            up_out[:, here] = up[:, there].astype(BF16)
            gate_out[:, here] = t_gate[pl.ds(t_index[sample], 1), there] + g_gate[pl.ds(g_index[sample], 1), there]
            at += width
        gout_out[:, pl.ds(features, 128)] = jnp.concatenate([glow, jnp.zeros((rows, 128 - rank), BF16)], 1)
        both = jnp.concatenate([contract_rows(glow, attn[...]), contract_rows(low, gout)], 0)
        terms = both.T.reshape(chips, span, 2 * rank)
        terms_out[...] = terms
        give_out[...] = terms.astype(BF16)

    shape = jax.ShapeDtypeStruct
    return call(
        kernel,
        (place, t_index, g_index, attn, cotangent, down_t, up, t_gate, g_gate),
        [SMEM_SPEC] * 3 + [VMEM_SPEC] * 6,
        [
            shape((1, features), F32),
            shape((rows, features + 128), BF16),
            shape((rows, rank), BF16),
            shape((rank, features), BF16),
            shape((rank, features), BF16),
            shape((chips, span, 2 * rank), F32),
            shape((chips, span, 2 * rank), BF16),
        ],
        [VMEM_SPEC] * 7,
        [pltpu.VMEM((rows, features), BF16)],
    )


def chunk(place, slot, block, width, terms, theirs, which):
    _, span, lanes = terms.shape
    shard = span // 2

    def kernel(place, block, terms, theirs, out):
        chip, rest = lax.div(place[slot], span), pl.ds(width, lanes)
        mine, other = half_rows(place[0], shard), half_rows(1 - place[0], shard)
        out[:, pl.ds(0, width)] = block[:, pl.ds(0, width)]
        if which == "first":
            out[mine, rest] = (terms[chip, mine, :] + theirs[chip, mine, :].astype(F32)).astype(BF16)
            out[other, rest] = jnp.zeros((shard, lanes), BF16)
        else:
            value = terms[chip] + theirs[chip].astype(F32) + block[:, rest].astype(F32)
            out[:, rest] = value.astype(BF16)

    return call(
        kernel, (place, block, terms, theirs), [SMEM_SPEC] + [VMEM_SPEC] * 3,
        jax.ShapeDtypeStruct((span, width + lanes), BF16), VMEM_SPEC, limit=8,
    )


def last_chunk(place, slot, block, second, width, terms, theirs):
    _, span, lanes = terms.shape
    shard, more = span // 2, second.shape[1]

    def kernel(place, block, second, terms, theirs, out):
        chip = lax.div(place[slot], span)
        mine, rest = half_rows(place[0], shard), pl.ds(width, lanes)
        value = (block[:, rest].astype(F32) + terms[chip] + theirs[chip].astype(F32)).astype(BF16)
        out[:, pl.ds(0, width)] = block[mine, pl.ds(0, width)]
        out[:, pl.ds(width, more)] = second[mine, :]
        out[:, pl.ds(width + more, lanes)] = value[:shard]
        out[:, pl.ds(width + more + lanes, lanes)] = value[shard:]

    return call(
        kernel, (place, block, second, terms, theirs), [SMEM_SPEC] + [VMEM_SPEC] * 4,
        jax.ShapeDtypeStruct((shard, width + more + 2 * lanes), BF16), VMEM_SPEC, limit=8,
    )


def side_step(place, distance, attn, gout, mates, down_t, rank, blocks, ring_blocks, x_block, totals, parts, grad_attn, gives, last):
    rows, features = attn.shape
    span = ring_blocks[0].shape[0]
    starts = [sum(blocks[:n]) for n in range(len(blocks))]
    names, args, specs, aliases = [], [], [], {}
    outs, out_specs = [], []

    def give(name, array, spec=VMEM_SPEC):
        names.append(name)
        args.append(array)
        specs.append(spec)

    def produce(name, shape, dtype, spec=VMEM_SPEC, old=None):
        if old is not None:
            aliases[len(args)] = len(outs)
            give(name + "_in", old, spec)
        outs.append((name, jax.ShapeDtypeStruct(shape, dtype)))
        out_specs.append(spec)

    give("place", place, SMEM_SPEC)
    give("attn", attn)
    give("gout", gout)
    give("attn_t", mates[0])
    give("gout_t", mates[1])
    give("down", down_t)
    for n, array in enumerate(ring_blocks):
        give(("ring", n), array)
    if x_block is not None:
        give("x", x_block)
        give("part_old", parts[0])
        give("part_t_old", parts[1])
    if last:
        for n, array in enumerate(gives):
            give(("given", n), array)
    produce("total", (rows, features), F32, old=totals[0])
    if last:
        give("total_t_in", totals[1])
        produce("send", (rows, features + (len(gives) + 2) * span), BF16)
    else:
        produce("total_t", (rows, features), F32, old=totals[1])
    produce("part", (rows, span), F32)
    if not last:
        produce("part_t", (rows, span), F32)
    if x_block is not None:
        produce("grad", (rows, features), BF16, HBM_SPEC, grad_attn)
    if x_block is not None and not last:
        produce("give", (rows, span), BF16)
    out_names = [name for name, _ in outs]

    def kernel(*refs):
        ref = dict(zip(names + [("out", name) for name in out_names], refs))
        grad_v, store = refs[len(names) + len(out_names) :]
        place = ref["place"]
        stores = []

        def put(src, dst):
            copy = pltpu.make_async_copy(src, dst, store.at[len(stores)])
            copy.start()
            stores.append(copy)

        def both(name, at):
            return jnp.concatenate([ref[name][:, at], ref[name + "_t"][:, at]], 0)

        def set_total_t(at, value):
            if last:
                ref[("out", "send")][:, at] = value.astype(BF16)
            else:
                ref[("out", "total_t")][:, at] = value

        if x_block is not None:
            at, there = cols(place[near(distance - 1)], span), pl.ds(starts[3], blocks[3])
            value = matmul(both("attn", at), ref["x"][...])
            ref[("out", "total")][:, there] = ref["total_in"][:, there] + value[:rows]
            value_t = value[rows:]
            if distance > 2:
                value_t = value_t + ref["total_t_in"][:, there]
            set_total_t(there, value_t)
            value = contract_cols(both("gout", there), ref["x"][...])
            grad_v[...] = (value[:rows] + ref["part_old"][...]).astype(BF16)
            put(grad_v, ref[("out", "grad")].at[:, at])
            value = (value[rows:] + ref["part_t_old"][...]).astype(BF16)
            if last:
                for n in range(len(gives)):
                    ref[("out", "send")][:, pl.ds(features + n * span, span)] = ref[("given", n)][...]
                ref[("out", "send")][:, pl.ds(features + len(gives) * span, span)] = value
            else:
                ref[("out", "give")][...] = value
        at = cols(place[near(distance)], span)
        glow = both("gout", pl.ds(features, rank))
        back = matmul(glow, ref["down"][:, at])
        a = both("attn", at)
        for n in range(3):
            there, width = pl.ds(starts[n], blocks[n]), blocks[n]
            piece = ref[("ring", n)][:, pl.ds(0, width)]
            value = matmul(a, piece)
            ref[("out", "total")][:, there] = ref["total_in"][:, there] + value[:rows]
            value_t = value[rows:]
            if distance > 1:
                value_t = value_t + ref["total_t_in"][:, there]
            set_total_t(there, value_t)
            back = back + contract_cols(both("gout", there), piece)
        ref[("out", "part")][...] = back[:rows]
        if last:
            ref[("out", "send")][:, pl.ds(features + (len(gives) + 1) * span, span)] = back[rows:].astype(BF16)
        else:
            ref[("out", "part_t")][...] = back[rows:]
        for copy in stores:
            copy.wait()

    result = call(
        kernel, args, specs, [shape for _, shape in outs], out_specs,
        [pltpu.VMEM((rows, span), BF16), pltpu.SemaphoreType.DMA((2,))], aliases, limit=STEP_LIMIT,
    )
    result = dict(zip(out_names, result))
    return (
        (result["total"], result.get("total_t")), (result["part"], result.get("part_t")), result.get("grad", grad_attn),
        result["send"] if last else result.get("give"),
    )


def step(place, jobs, attn, blocks, grads, total=None, add=None, final=None, updated=None, grad_attn=None, extra=None, sums=None):
    rows, features = attn.shape
    gout, down_t, rank = grads
    place_span = span_of(jobs)
    starts = [sum(blocks[:n]) for n in range(len(blocks))]
    names, args, specs, aliases = [], [], [], {}

    def give(name, array, spec=VMEM_SPEC):
        names.append(name)
        args.append(array)
        specs.append(spec)

    give("place", place, SMEM_SPEC)
    give("attn", attn)
    give("gout", gout)
    if any(job["part"] is None for job in jobs):
        give("down", down_t)
    if extra is not None:
        give("extra", extra[0])
    if add is not None:
        give("low", add[0])
        give("up", add[1])
    if any(job["final"] for job in jobs):
        give("resid", final[0], HBM_SPEC)
        give("gate", final[1])
    outs, out_specs = [], []

    def produce(name, shape, dtype, spec, old=None):
        if old is not None:
            aliases[len(args)] = len(outs)
            give(name + "_in", old, spec)
        outs.append((name, jax.ShapeDtypeStruct(shape, dtype)))
        out_specs.append(spec)

    if not all(job["final"] for job in jobs):
        produce("total", (rows, features), F32, VMEM_SPEC, total)
    elif total is not None:
        give("total_in", total)
    if any(job["final"] for job in jobs):
        produce("updated", (rows, features), BF16, HBM_SPEC, updated)
    if not all(job["open"] for job in jobs):
        produce("grad", (rows, features), BF16, HBM_SPEC, grad_attn)
    if sums is not None:
        for n, array in enumerate(sums[:4]):
            give(("sums", n), array)
        lanes = sums[0].shape[2]
        for n in range(2):
            produce(("sums", n), (lanes // 2, span_of(jobs) // 2), F32, VMEM_SPEC)
    scratch = []
    tiny = pltpu.VMEM((16, 128), BF16)
    for j, job in enumerate(jobs):
        some = job["pieces"][0][0]
        job["halves"] = halves = isinstance(some, tuple)
        job["span"] = span = place_span
        job["width"] = width = sum(blocks[n] for n in job["blocks"])
        job["deep"] = deep = span * len(job["chips"])
        for n, per in enumerate(job["pieces"]):
            for c, array in enumerate(per):
                for h, half in enumerate(array if halves else (array,)):
                    give(("piece", j, n, c, h), half.array if isinstance(half, Part) else half)
        if job["part"] is not None:
            for c, array in enumerate(job["part"]):
                if array is not None:
                    give(("part", j, c), array)
        if job["open"]:
            produce(("open", j), (rows, deep), F32, VMEM_SPEC)
        scratch += [
            pltpu.VMEM((deep, width), BF16) if halves else tiny,
            pltpu.VMEM((rows, width), BF16) if job["final"] else tiny,
            pltpu.VMEM((rows, width), BF16) if job["final"] else tiny,
            tiny if job["open"] else pltpu.VMEM((rows, deep), BF16),
        ]
    n_job = len(scratch)
    scratch += [pltpu.SemaphoreType.DMA((8,)), pltpu.SemaphoreType.DMA((8,))]
    out_names = [name for name, _ in outs]

    def kernel(*refs):
        ref = dict(zip(names + [("out", name) for name in out_names], refs))
        rest = refs[len(names) + len(out_names) :]
        load, store = rest[n_job:]
        place = ref["place"]
        loads, stores = {}, []

        def put(src, dst):
            copy = pltpu.make_async_copy(src, dst, store.at[len(stores)])
            copy.start()
            stores.append(copy)

        for j, job in enumerate(jobs):
            if job["final"]:
                for block in job["blocks"]:
                    here = pl.ds(starts[block] - starts[job["blocks"][0]], blocks[block])
                    src = ref["resid"].at[:, cols(place[2 + block], blocks[block])]
                    loads[j, block] = pltpu.make_async_copy(src, rest[4 * j + 1].at[:, here], load.at[len(loads)])
                    loads[j, block].start()
        if extra is not None and extra[1] is not None:
            span = jobs[0]["span"]
            for n, slot in enumerate(extra[1]):
                put(ref["extra"].at[:, pl.ds(features + n * span, span)], ref[("out", "grad")].at[:, cols(place[slot], span)])
        for j, job in enumerate(jobs):
            frozen_v, resid_v, result_v, back_v = rest[4 * j : 4 * j + 4]
            span = job["span"]
            chip_cols = [cols(place[s], span) for s in job["chips"]]
            back = [None] * len(chip_cols)
            for n, block in enumerate(job["blocks"]):
                width = blocks[block]
                here, there = pl.ds(starts[block] - starts[job["blocks"][0]], width), pl.ds(starts[block], width)
                value = ref["total_in"][:, there] if total is not None else matmul(ref["low"][...], ref["up"][:, there])
                if extra is not None:
                    value = value + ref["extra"][:, there].astype(F32)
                for c, at in enumerate(chip_cols):
                    if job["halves"]:
                        shard = span // 2
                        for h, core in enumerate((place[0], 1 - place[0])):
                            to = pl.ds(pl.multiple_of(c * span + core * shard, 16), shard)
                            half = job["pieces"][n][c][h]
                            row, col = (half.row, half.col) if isinstance(half, Part) else (0, 0)
                            frozen_v[to, here] = ref[("piece", j, n, c, h)][pl.ds(row, shard), pl.ds(col, width)]
                        piece = frozen_v[pl.ds(c * span, span), here]
                    else:
                        piece = ref[("piece", j, n, c, 0)][pl.ds(0, span), :]
                    value = value + matmul(ref["attn"][:, at], piece)
                    term = contract_cols(ref["gout"][:, there], piece)
                    back[c] = term if back[c] is None else back[c] + term
                if job["final"]:
                    loads[j, block].wait()
                    result_v[:, here] = (resid_v[:, here].astype(F32) + ref["gate"][:, there] * value).astype(BF16)
                    put(result_v.at[:, here], ref[("out", "updated")].at[:, cols(place[2 + block], width)])
                else:
                    ref[("out", "total")][:, there] = value
            for c, at in enumerate(chip_cols):
                mine = pl.ds(c * span, span)
                if job["part"] is None:
                    value = back[c] + matmul(ref["gout"][:, pl.ds(features, rank)], ref["down"][:, at])
                else:
                    from_mate = job["part"][c] is None
                    part = ref["extra"][:, pl.ds(features + len(extra[1]) * span, span)].astype(F32) if from_mate else ref[("part", j, c)][...]
                    value = back[c] + part
                if job["open"]:
                    ref[("out", ("open", j))][:, mine] = value
                else:
                    back_v[:, mine] = value.astype(BF16)
                    put(back_v.at[:, mine], ref[("out", "grad")].at[:, at])
        if sums is not None:
            span = jobs[0]["span"]
            chip, mine = lax.div(place[OWN], span), half_rows(place[0], span // 2)
            rest = cols(sums[4] + place[0] * lanes, lanes)
            value = ref[("sums", 0)][chip, mine, :] + ref[("sums", 1)][chip, mine, :].astype(F32)
            value = value + ref[("sums", 2)][:, rest].astype(F32) + ref[("sums", 3)][:, rest].astype(F32)
            value = (sums[5] * value).T
            ref[("out", ("sums", 0))][...] = value[: lanes // 2]
            ref[("out", ("sums", 1))][...] = value[lanes // 2 :]
        for copy in stores:
            copy.wait()

    result = call(
        kernel, args, specs, [shape for _, shape in outs], out_specs, scratch, aliases,
        weight=12, limit=STEP_LIMIT,
    )
    result = dict(zip(out_names, result))
    opened = [result[("open", j)] for j, job in enumerate(jobs) if job["open"]]
    if sums is not None:
        opened += [result[("sums", n)] for n in range(2)]
    return result.get("total", total), result.get("updated", updated), result.get("grad", grad_attn), *opened


class Part:
    def __init__(self, array, row=0, col=0):
        self.array, self.row, self.col = array, row, col


def span_of(jobs):
    sizes = []
    for job in jobs:
        some = job["pieces"][0][0]
        sizes.append(2 * some[0].shape[0] if isinstance(some, tuple) else some.shape[0])
    return min(sizes)


def job(chips, blocks, pieces, part=None, open=False, final=False):
    return dict(chips=chips, blocks=blocks, pieces=pieces, part=part, open=open, final=final)


EDGES = dict(
    gout="s",
    k0="s",
    r1="T",
    x1="T",
    q1="rTm",
    s2="Tx",
    k2="x",
    r3="S",
    x3="S",
    q3="Tx",
    s3="Tx",
    k3="x",
    r4="TX",
    x4="s",
    q4="rT",
    send="r",
    q5="e",
)
WHEN = "srs"


def after(value, *others):
    return lax.optimization_barrier((value, *others))[0]


def ring_body(
    table,
    attn,
    resid,
    frozen,
    adapter_down_weight,
    adapter_up_weight,
    timestep_gate,
    guidance_gate,
    timestep_index,
    guidance_index,
    cotangent,
):
    rows, features = attn.shape
    axis_size = lax.axis_size("blk")
    chips = axis_size // 2
    blocks = blocks_of(features)
    me = lax.axis_index("blk")
    device = lax.axis_index("groups") * axis_size + me
    core_pairs = [(i, i ^ 1) for i in range(axis_size)]
    ring = functools.partial(lax.ppermute, axis_name="blk", perm=ring_pairs(chips))
    swap = functools.partial(lax.ppermute, axis_name="blk", perm=core_pairs)
    cross = functools.partial(lax.ppermute, axis_name="groups", perm=[(0, 1), (1, 0)])
    place = lax.dynamic_index_in_dim(jnp.asarray(table), device, 0, False)

    rank = adapter_up_weight.shape[0]
    steps = chips // 2 - 1
    far = near(steps + 1)
    wide = blocks[1]
    def gate(name, value, **have):
        others = [have[k] for k in EDGES.get(name, "") if have.get(k) is not None]
        return after(value, *others) if others else value

    theirs = swap(frozen)
    own = pair(place, cut(place, frozen, blocks), theirs, blocks, [0, 1, 2, 3])
    r, q, s = [None, ring(own[0])], [None], [None, ring(own[2])]
    known = dict(o=own[0], p=own[1], r=r[1], s=s[1])
    attn_t = known["a"] = swap(gate("attn", attn, **known))
    gate_row, gout, low, up, down_t, terms, given = adapter(
        place, timestep_index, guidance_index, attn, gate("adapter", cotangent, **known),
        adapter_down_weight.T, adapter_up_weight, timestep_gate, guidance_gate, blocks, chips,
    )
    terms_t = known["t"] = swap(given)
    first_q = known["f"] = chunk(place, far, own[1], wide, terms, terms_t, "first")
    q.append(ring(first_q))
    known["q"] = q[1]
    gout_t = known["m"] = swap(gate("gout", gout, **known))
    grads = (gout, down_t, rank)
    total, _, grad_attn = step(
        place, [job([OWN], [0, 1, 2, 3], [[block] for block in own])], attn, blocks,
        (gate("k0", gout, **known), down_t, rank), add=(low, up),
    )
    totals, parts, give, gives, x = (total, None), None, None, [], [None]

    def run(n, arrival, **have):
        nonlocal totals, parts, grad_attn, give
        last = n == steps
        totals, parts, grad_attn, give = side_step(
            place, n, attn, gate(f"k{n}", after(gout, arrival), **have), (attn_t, gout_t), down_t, rank, blocks,
            [r[n], q[n], s[n]], x[n - 1], totals, parts, grad_attn, gives, last,
        )
        if give is not None and not last:
            gives.append(give)

    for n in range(1, steps + 1):
        last = n == steps
        prev = dict(T=totals[0], x=x[n - 1], S=s[n - 1], Q=q[n - 1])
        r[n] = gate(f"r{n}", r[n], **{**known, **prev})
        r.append(ring(own_half(place, r[n]) if last else r[n]))
        x.append(cross(gate(f"x{n}", r[n], **prev)))
        if n > 1 and WHEN[n - 2] == "r":
            run(n - 1, r[n], x=x[n - 1], X=x[n - 2])
        q[n] = gate(f"q{n}", q[n], **{**known, "r": r[n], "T": totals[0], "x": x[n - 1]})
        if not last:
            message = chunk(place, across(steps + 1 - n), q[n], wide, terms, terms_t, "middle")
            q.append(ring(message))
        if n > 1 and WHEN[n - 2] == "q":
            run(n - 1, q[n], x=x[n - 1], X=x[n - 2], c=message)
        s[n] = gate(f"s{n}", s[n], **{**known, "q": q[n], "r": r[n], "T": totals[0], "x": x[n - 1]})
        if last:
            message = last_chunk(place, across(1), q[n], s[n], wide, terms, terms_t)
            q.append(ring(message))
        else:
            s.append(ring(s[n]))
        if WHEN[n - 1] == "s":
            run(n, s[n], x=x[n - 1], c=message)

    r_far = gate("r4", r[steps + 1], X=x[steps], T=totals[0], s=s[steps], q=q[steps])
    x_far = cross(gate("x4", r_far, X=x[steps], T=totals[0], s=s[steps]))
    if WHEN[steps - 1] == "r":
        run(steps, r_far, X=x[steps], c=message)
    x_before = gate("back", x[steps], r=r_far)
    x_swapped, r_swapped = swap(x_before), swap(r_far)
    swaps = dict(v=x_swapped, w=r_swapped)
    q_far = gate("q4", q[steps + 1], r=r_far, T=totals[0], **swaps)
    if WHEN[steps - 1] == "q":
        run(steps, q_far, X=x[steps], c=message)
    extra = swap(gate("send", give, r=r_far, X=x[steps], q=q_far))
    q_swapped = swap(gate("q5", q_far, e=extra, **swaps))
    x_job = job([near(steps), across(steps)], [3], [[x_before, x_swapped]], part=[parts[0], None])
    q_piece, s_piece = (q_far, q_swapped), (Part(q_far, 0, wide), Part(q_swapped, 0, wide))
    columns = [across(n) for n in range(1, steps)]
    far_job = job([far], [0, 1, 2], [[(r_far, r_swapped)], [q_piece], [s_piece]], open=True, final=True)
    total, updated, grad_attn, part = step(
        place, [x_job, far_job], attn, blocks, grads, total=totals[0], final=(resid, gate_row), grad_attn=grad_attn,
        extra=(extra, columns),
    )
    x_far = gate("x5", x_far, s=q_far, q=q_far, T=total)
    sums = (terms, terms_t, q_far, q_swapped, wide + blocks[2], float(rows * axis_size) ** (-0.5))
    _, updated, grad_attn, grad_down_t, grad_up = step(
        place, [job([far], [3], [[(x_far, swap(x_far))]], part=[part], final=True)],
        attn, blocks, grads, total=total, final=(resid, gate_row), updated=updated, grad_attn=grad_attn, sums=sums,
    )
    return updated, grad_attn, grad_down_t.T, grad_up.T


def gather_body(
    attn,
    resid,
    frozen,
    adapter_down_weight,
    adapter_up_weight,
    timestep_gate,
    guidance_gate,
    timestep_index,
    guidance_index,
    cotangent,
):
    rows, features = attn.shape
    axis_size = lax.axis_size("blk")
    whole = lax.all_gather(frozen, "blk", axis=0, tiled=True)
    sample = (lax.axis_index("blk") * rows + jnp.arange(rows, dtype=jnp.int32)) // IMAGE_TOKENS
    gate = timestep_gate[timestep_index[sample]] + guidance_gate[guidance_index[sample]]
    down_half = adapter_down_weight.astype(BF16)
    up_half = adapter_up_weight.astype(BF16)
    low = matmul(attn, down_half).astype(BF16)
    gout = (gate * cotangent.astype(F32)).astype(BF16)
    glow = contract_cols(gout, up_half).astype(BF16)
    terms = jnp.concatenate([contract_rows(attn, glow), contract_rows(gout, low)], 1)
    summed = lax.psum_scatter(terms, "blk", scatter_dimension=0, tiled=True)
    grad_scale = float(rows * axis_size) ** (-0.5)
    rank = glow.shape[1]
    base = matmul(attn, whole) + matmul(low, up_half)
    updated = (resid.astype(F32) + gate * base).astype(BF16)
    grad_attn = (contract_cols(gout, whole) + contract_cols(glow, down_half)).astype(BF16)
    return updated, grad_attn, grad_scale * summed[:, :rank], grad_scale * summed[:, rank:]


def solution(mesh):
    def run(attn, resid, frozen, *rest):
        axis_size, groups = mesh.shape["blk"], mesh.shape["groups"]
        rows, span = attn.shape[0] // (axis_size * groups), 2 * frozen.shape[0] // axis_size
        by_ring = groups == 2 and axis_size == 16
        by_ring = by_ring and span % 128 == 0 and frozen.shape[1] % 3072 == 0 and IMAGE_TOKENS % rows == 0
        body = gather_body
        if by_ring:
            table = place_table(groups, axis_size, rows, span, frozen.shape[1])
            body = functools.partial(ring_body, table)
        spec = P(("groups", "blk"), None)
        return jax.shard_map(
            body,
            mesh=mesh,
            in_specs=(spec, spec, P("blk", None), P(), P(), P(), P(), P("groups"), P("groups"), spec),
            out_specs=(spec, spec, spec, spec),
            check_vma=False,
        )(attn, resid, frozen, *rest)

    return run
```

```python
import functools

import jax
import jax.numpy as jnp
import numpy as np
from jax import lax
from jax.experimental import pallas as pl
from jax.experimental.pallas import tpu as pltpu
from jax.sharding import PartitionSpec as P

IMAGE_TOKENS = 4096
F32 = jnp.float32
BF16 = jnp.bfloat16


def contract_rows(left, right):
    return lax.dot_general(left, right, (((0,), (0,)), ((), ())), preferred_element_type=F32)


def contract_cols(left, right):
    return lax.dot_general(left, right, (((1,), (1,)), ((), ())), preferred_element_type=F32)


def matmul(left, right):
    return jnp.dot(left, right, preferred_element_type=F32)


def ring_order(chips):
    return [0] + list(range(1, chips, 2)) + list(range(chips - 2, 0, -2))


def ring_pairs(chips):
    order = ring_order(chips)
    pairs = []
    for place, chip in enumerate(order):
        after, before = order[(place + 1) % chips], order[(place - 1) % chips]
        pairs += [(2 * chip, 2 * after), (2 * chip + 1, 2 * before + 1)]
    return pairs


WIDTHS = (7, 4, 6, 7)
OWN = 6


def near(distance):
    return 5 + 2 * distance


def across(distance):
    return 6 + 2 * distance


def blocks_of(features):
    lane = features // 24
    return tuple(width * lane for width in WIDTHS)


def place_table(groups, axis_size, rows, span, features):
    chips = axis_size // 2
    order = ring_order(chips)
    wide, middle, third, _ = blocks_of(features)
    table = []
    for g in range(groups):
        for b in range(axis_size):
            chip, core = divmod(b, 2)
            at, toward = order.index(chip), 2 * core - 1
            far_side = wide + middle + third
            own, others = (0, far_side) if g == 0 else (far_side, 0)
            line = [core, b * rows // IMAGE_TOKENS, own, wide, wide + middle, others, chip * span]
            for n in range(1, chips // 2):
                line += [order[(at + toward * n) % chips] * span, order[(at - toward * n) % chips] * span]
            table.append(line + [order[(at + chips // 2) % chips] * span])
    return np.asarray(table, np.int32)


STEP_LIMIT = 16
VMEM_SPEC = pl.BlockSpec(memory_space=pltpu.VMEM)
SMEM_SPEC = pl.BlockSpec(memory_space=pltpu.SMEM)
HBM_SPEC = pl.BlockSpec(memory_space=pltpu.HBM)


def cols(start, width):
    return pl.ds(pl.multiple_of(start, 128), width)


def half_rows(core, shard):
    return pl.ds(pl.multiple_of(core * shard, 16), shard)


def call(kernel, args, specs, out_shape, out_specs, scratch=(), aliases=None, weight=1, limit=16):
    return pl.pallas_call(
        kernel,
        in_specs=specs,
        out_shape=out_shape,
        out_specs=out_specs,
        scratch_shapes=scratch,
        input_output_aliases=aliases or {},
        compiler_params=pltpu.CompilerParams(vmem_limit_bytes=limit * 1024 * 1024),
        cost_estimate=pl.CostEstimate(flops=0, bytes_accessed=weight, transcendentals=0),
    )(*args)


def cut(place, frozen, blocks):
    shard = frozen.shape[0]

    def kernel(place, frozen, *refs):
        outs, sems = refs[:-1], refs[-1]
        copies = []
        for n, width in enumerate(blocks):
            copies.append(pltpu.make_async_copy(frozen.at[:, cols(place[2 + n], width)], outs[n], sems.at[n]))
            copies[n].start()
        for copy in copies:
            copy.wait()

    return call(
        kernel, (place, frozen), [SMEM_SPEC, HBM_SPEC], [jax.ShapeDtypeStruct((shard, w), BF16) for w in blocks],
        [VMEM_SPEC] * len(blocks), [pltpu.SemaphoreType.DMA((len(blocks),))], limit=4,
    )


def pair(place, mine, theirs, blocks, which):
    shard = theirs.shape[0]

    def kernel(place, *refs):
        theirs, refs = refs[len(which)], refs[: len(which)] + refs[len(which) + 1 :]
        for n, block in enumerate(which):
            out = refs[len(which) + n]
            out[half_rows(place[0], shard), :] = refs[n][...]
            out[half_rows(1 - place[0], shard), :] = theirs[:, cols(place[2 + block], blocks[block])]

    return call(
        kernel, (place, *[mine[block] for block in which], theirs), [SMEM_SPEC] + [VMEM_SPEC] * (len(which) + 1),
        [jax.ShapeDtypeStruct((2 * shard, blocks[block]), BF16) for block in which], [VMEM_SPEC] * len(which), limit=4,
    )


def own_half(place, whole):
    shard, width = whole.shape[0] // 2, whole.shape[1]

    def kernel(place, whole, out):
        out[...] = whole[half_rows(place[0], shard), :]

    return call(
        kernel, (place, whole), [SMEM_SPEC, VMEM_SPEC], jax.ShapeDtypeStruct((shard, width), BF16), VMEM_SPEC, limit=4,
    )


def adapter(place, t_index, g_index, attn, cotangent, down_t, up, t_gate, g_gate, blocks, chips):
    rows, features = attn.shape
    rank = up.shape[0]
    span = features // chips

    def kernel(place, t_index, g_index, attn, cotangent, down_t, up, t_gate, g_gate,
               gate_out, gout_out, low_out, up_out, down_out, terms_out, give_out, gout_v):
        sample = place[1]
        gate = t_gate[pl.ds(t_index[sample], 1), :] + g_gate[pl.ds(g_index[sample], 1), :]
        gout = (gate * cotangent[...].astype(F32)).astype(BF16)
        gout_v[...] = gout
        up_half = up[...].astype(BF16)
        down_half = down_t[...].astype(BF16)
        down_out[...] = down_half
        low = contract_cols(attn[...], down_half).astype(BF16)
        glow = contract_cols(gout, up_half).astype(BF16)
        low_out[...] = low
        at = 0
        for n, width in enumerate(blocks):
            here, there = pl.ds(at, width), cols(place[2 + n], width)
            gout_out[:, here] = gout_v[:, there]
            up_out[:, here] = up[:, there].astype(BF16)
            gate_out[:, here] = t_gate[pl.ds(t_index[sample], 1), there] + g_gate[pl.ds(g_index[sample], 1), there]
            at += width
        gout_out[:, pl.ds(features, 128)] = jnp.concatenate([glow, jnp.zeros((rows, 128 - rank), BF16)], 1)
        both = jnp.concatenate([contract_rows(glow, attn[...]), contract_rows(low, gout)], 0)
        terms = both.T.reshape(chips, span, 2 * rank)
        terms_out[...] = terms
        give_out[...] = terms.astype(BF16)

    shape = jax.ShapeDtypeStruct
    return call(
        kernel,
        (place, t_index, g_index, attn, cotangent, down_t, up, t_gate, g_gate),
        [SMEM_SPEC] * 3 + [VMEM_SPEC] * 6,
        [
            shape((1, features), F32),
            shape((rows, features + 128), BF16),
            shape((rows, rank), BF16),
            shape((rank, features), BF16),
            shape((rank, features), BF16),
            shape((chips, span, 2 * rank), F32),
            shape((chips, span, 2 * rank), BF16),
        ],
        [VMEM_SPEC] * 7,
        [pltpu.VMEM((rows, features), BF16)],
    )


def chunk(place, slot, block, width, terms, theirs, which):
    _, span, lanes = terms.shape
    shard = span // 2

    def kernel(place, block, terms, theirs, out):
        chip, rest = lax.div(place[slot], span), pl.ds(width, lanes)
        mine, other = half_rows(place[0], shard), half_rows(1 - place[0], shard)
        out[:, pl.ds(0, width)] = block[:, pl.ds(0, width)]
        if which == "first":
            out[mine, rest] = (terms[chip, mine, :] + theirs[chip, mine, :].astype(F32)).astype(BF16)
            out[other, rest] = jnp.zeros((shard, lanes), BF16)
        else:
            value = terms[chip] + theirs[chip].astype(F32) + block[:, rest].astype(F32)
            out[:, rest] = value.astype(BF16)

    return call(
        kernel, (place, block, terms, theirs), [SMEM_SPEC] + [VMEM_SPEC] * 3,
        jax.ShapeDtypeStruct((span, width + lanes), BF16), VMEM_SPEC, limit=8,
    )


def last_chunk(place, slot, block, second, width, terms, theirs):
    _, span, lanes = terms.shape
    shard, more = span // 2, second.shape[1]

    def kernel(place, block, second, terms, theirs, out):
        chip = lax.div(place[slot], span)
        mine, rest = half_rows(place[0], shard), pl.ds(width, lanes)
        value = (block[:, rest].astype(F32) + terms[chip] + theirs[chip].astype(F32)).astype(BF16)
        out[:, pl.ds(0, width)] = block[mine, pl.ds(0, width)]
        out[:, pl.ds(width, more)] = second[mine, :]
        out[:, pl.ds(width + more, lanes)] = value[:shard]
        out[:, pl.ds(width + more + lanes, lanes)] = value[shard:]

    return call(
        kernel, (place, block, second, terms, theirs), [SMEM_SPEC] + [VMEM_SPEC] * 4,
        jax.ShapeDtypeStruct((shard, width + more + 2 * lanes), BF16), VMEM_SPEC, limit=8,
    )


def side_step(place, distance, attn, gout, mates, down_t, rank, blocks, ring_blocks, x_block, totals, parts, grad_attn, gives, last):
    rows, features = attn.shape
    span = ring_blocks[0].shape[0]
    starts = [sum(blocks[:n]) for n in range(len(blocks))]
    names, args, specs, aliases = [], [], [], {}
    outs, out_specs = [], []

    def give(name, array, spec=VMEM_SPEC):
        names.append(name)
        args.append(array)
        specs.append(spec)

    def produce(name, shape, dtype, spec=VMEM_SPEC, old=None):
        if old is not None:
            aliases[len(args)] = len(outs)
            give(name + "_in", old, spec)
        outs.append((name, jax.ShapeDtypeStruct(shape, dtype)))
        out_specs.append(spec)

    give("place", place, SMEM_SPEC)
    give("attn", attn)
    give("gout", gout)
    give("attn_t", mates[0])
    give("gout_t", mates[1])
    give("down", down_t)
    for n, array in enumerate(ring_blocks):
        give(("ring", n), array)
    if x_block is not None:
        give("x", x_block)
        give("part_old", parts[0])
        give("part_t_old", parts[1])
    if last:
        for n, array in enumerate(gives):
            give(("given", n), array)
    produce("total", (rows, features), F32, old=totals[0])
    if last:
        give("total_t_in", totals[1])
        produce("send", (rows, features + (len(gives) + 2) * span), BF16)
    else:
        produce("total_t", (rows, features), F32, old=totals[1])
    produce("part", (rows, span), F32)
    if not last:
        produce("part_t", (rows, span), F32)
    if x_block is not None:
        produce("grad", (rows, features), BF16, HBM_SPEC, grad_attn)
    if x_block is not None and not last:
        produce("give", (rows, span), BF16)
    out_names = [name for name, _ in outs]

    def kernel(*refs):
        ref = dict(zip(names + [("out", name) for name in out_names], refs))
        grad_v, store = refs[len(names) + len(out_names) :]
        place = ref["place"]
        stores = []

        def put(src, dst):
            copy = pltpu.make_async_copy(src, dst, store.at[len(stores)])
            copy.start()
            stores.append(copy)

        def both(name, at):
            return jnp.concatenate([ref[name][:, at], ref[name + "_t"][:, at]], 0)

        def set_total_t(at, value):
            if last:
                ref[("out", "send")][:, at] = value.astype(BF16)
            else:
                ref[("out", "total_t")][:, at] = value

        if x_block is not None:
            at, there = cols(place[near(distance - 1)], span), pl.ds(starts[3], blocks[3])
            value = matmul(both("attn", at), ref["x"][...])
            ref[("out", "total")][:, there] = ref["total_in"][:, there] + value[:rows]
            value_t = value[rows:]
            if distance > 2:
                value_t = value_t + ref["total_t_in"][:, there]
            set_total_t(there, value_t)
            value = contract_cols(both("gout", there), ref["x"][...])
            grad_v[...] = (value[:rows] + ref["part_old"][...]).astype(BF16)
            put(grad_v, ref[("out", "grad")].at[:, at])
            value = (value[rows:] + ref["part_t_old"][...]).astype(BF16)
            if last:
                for n in range(len(gives)):
                    ref[("out", "send")][:, pl.ds(features + n * span, span)] = ref[("given", n)][...]
                ref[("out", "send")][:, pl.ds(features + len(gives) * span, span)] = value
            else:
                ref[("out", "give")][...] = value
        at = cols(place[near(distance)], span)
        glow = both("gout", pl.ds(features, rank))
        back = matmul(glow, ref["down"][:, at])
        a = both("attn", at)
        for n in range(3):
            there, width = pl.ds(starts[n], blocks[n]), blocks[n]
            piece = ref[("ring", n)][:, pl.ds(0, width)]
            value = matmul(a, piece)
            ref[("out", "total")][:, there] = ref["total_in"][:, there] + value[:rows]
            value_t = value[rows:]
            if distance > 1:
                value_t = value_t + ref["total_t_in"][:, there]
            set_total_t(there, value_t)
            back = back + contract_cols(both("gout", there), piece)
        ref[("out", "part")][...] = back[:rows]
        if last:
            ref[("out", "send")][:, pl.ds(features + (len(gives) + 1) * span, span)] = back[rows:].astype(BF16)
        else:
            ref[("out", "part_t")][...] = back[rows:]
        for copy in stores:
            copy.wait()

    result = call(
        kernel, args, specs, [shape for _, shape in outs], out_specs,
        [pltpu.VMEM((rows, span), BF16), pltpu.SemaphoreType.DMA((2,))], aliases, limit=STEP_LIMIT,
    )
    result = dict(zip(out_names, result))
    return (
        (result["total"], result.get("total_t")), (result["part"], result.get("part_t")), result.get("grad", grad_attn),
        result["send"] if last else result.get("give"),
    )


def step(place, jobs, attn, blocks, grads, total=None, add=None, final=None, updated=None, grad_attn=None, extra=None, sums=None):
    rows, features = attn.shape
    gout, down_t, rank = grads
    place_span = span_of(jobs)
    starts = [sum(blocks[:n]) for n in range(len(blocks))]
    names, args, specs, aliases = [], [], [], {}

    def give(name, array, spec=VMEM_SPEC):
        names.append(name)
        args.append(array)
        specs.append(spec)

    give("place", place, SMEM_SPEC)
    give("attn", attn)
    give("gout", gout)
    if any(job["part"] is None for job in jobs):
        give("down", down_t)
    if extra is not None:
        give("extra", extra[0])
    if add is not None:
        give("low", add[0])
        give("up", add[1])
    if any(job["final"] for job in jobs):
        if not all(job["folded"] for job in jobs):
            give("resid", final[0], HBM_SPEC)
        give("gate", final[1])
    outs, out_specs = [], []

    def produce(name, shape, dtype, spec, old=None):
        if old is not None:
            aliases[len(args)] = len(outs)
            give(name + "_in", old, spec)
        outs.append((name, jax.ShapeDtypeStruct(shape, dtype)))
        out_specs.append(spec)

    if not all(job["final"] for job in jobs):
        produce("total", (rows, features), F32, VMEM_SPEC, total)
    elif total is not None:
        give("total_in", total)
    if any(job["final"] for job in jobs):
        produce("updated", (rows, features), BF16, HBM_SPEC, updated)
    if not all(job["open"] for job in jobs):
        produce("grad", (rows, features), BF16, HBM_SPEC, grad_attn)
    if sums is not None:
        for n, array in enumerate(sums[:4]):
            give(("sums", n), array)
        lanes = sums[0].shape[2]
        for n in range(2):
            produce(("sums", n), (lanes // 2, span_of(jobs) // 2), F32, VMEM_SPEC)
    scratch = []
    tiny = pltpu.VMEM((16, 128), BF16)
    for j, job in enumerate(jobs):
        some = job["pieces"][0][0]
        job["halves"] = halves = isinstance(some, tuple)
        job["span"] = span = place_span
        job["width"] = width = sum(blocks[n] for n in job["blocks"])
        job["deep"] = deep = span * len(job["chips"])
        for n, per in enumerate(job["pieces"]):
            for c, array in enumerate(per):
                for h, half in enumerate(array if halves else (array,)):
                    give(("piece", j, n, c, h), half.array if isinstance(half, Part) else half)
        if job["part"] is not None:
            for c, array in enumerate(job["part"]):
                if array is not None:
                    give(("part", j, c), array)
        if job["open"]:
            produce(("open", j), (rows, deep), F32, VMEM_SPEC)
        scratch += [
            pltpu.VMEM((deep, width), BF16) if halves else tiny,
            pltpu.VMEM((rows, width), BF16) if job["final"] != job["folded"] else tiny,
            pltpu.VMEM((rows, width), BF16) if job["final"] else tiny,
            tiny if job["open"] else pltpu.VMEM((rows, deep), BF16),
        ]
    n_job = len(scratch)
    scratch += [pltpu.SemaphoreType.DMA((8,)), pltpu.SemaphoreType.DMA((8,))]
    out_names = [name for name, _ in outs]

    def kernel(*refs):
        ref = dict(zip(names + [("out", name) for name in out_names], refs))
        rest = refs[len(names) + len(out_names) :]
        load, store = rest[n_job:]
        place = ref["place"]
        loads, stores = {}, []

        def put(src, dst):
            copy = pltpu.make_async_copy(src, dst, store.at[len(stores)])
            copy.start()
            stores.append(copy)

        for j, job in enumerate(jobs):
            if job["final"] != job["folded"]:
                for block in job["blocks"]:
                    here = pl.ds(starts[block] - starts[job["blocks"][0]], blocks[block])
                    src = ref["resid"].at[:, cols(place[2 + block], blocks[block])]
                    loads[j, block] = pltpu.make_async_copy(src, rest[4 * j + 1].at[:, here], load.at[len(loads)])
                    loads[j, block].start()
        if extra is not None and extra[1] is not None:
            span = jobs[0]["span"]
            for n, slot in enumerate(extra[1]):
                put(ref["extra"].at[:, pl.ds(features + n * span, span)], ref[("out", "grad")].at[:, cols(place[slot], span)])
        for j, job in enumerate(jobs):
            frozen_v, resid_v, result_v, back_v = rest[4 * j : 4 * j + 4]
            span = job["span"]
            chip_cols = [cols(place[s], span) for s in job["chips"]]
            back = [None] * len(chip_cols)
            for n, block in enumerate(job["blocks"]):
                width = blocks[block]
                here, there = pl.ds(starts[block] - starts[job["blocks"][0]], width), pl.ds(starts[block], width)
                if job["final"] and job["folded"]:
                    value = 0.0
                else:
                    value = ref["total_in"][:, there] if total is not None else matmul(ref["low"][...], ref["up"][:, there])
                if extra is not None:
                    value = value + ref["extra"][:, there].astype(F32)
                for c, at in enumerate(chip_cols):
                    if job["halves"]:
                        shard = span // 2
                        for h, core in enumerate((place[0], 1 - place[0])):
                            to = pl.ds(pl.multiple_of(c * span + core * shard, 16), shard)
                            half = job["pieces"][n][c][h]
                            row, col = (half.row, half.col) if isinstance(half, Part) else (0, 0)
                            frozen_v[to, here] = ref[("piece", j, n, c, h)][pl.ds(row, shard), pl.ds(col, width)]
                        piece = frozen_v[pl.ds(c * span, span), here]
                    else:
                        piece = ref[("piece", j, n, c, 0)][pl.ds(0, span), :]
                    value = value + matmul(ref["attn"][:, at], piece)
                    term = contract_cols(ref["gout"][:, there], piece)
                    back[c] = term if back[c] is None else back[c] + term
                if job["final"]:
                    if job["folded"]:
                        start = ref["total_in"][:, there]
                    else:
                        loads[j, block].wait()
                        start = resid_v[:, here].astype(F32)
                    result_v[:, here] = (start + ref["gate"][:, there] * value).astype(BF16)
                    put(result_v.at[:, here], ref[("out", "updated")].at[:, cols(place[2 + block], width)])
                else:
                    if job["folded"]:
                        loads[j, block].wait()
                        value = resid_v[:, here].astype(F32) + ref["gate"][:, there] * value
                    ref[("out", "total")][:, there] = value
            for c, at in enumerate(chip_cols):
                mine = pl.ds(c * span, span)
                if job["part"] is None:
                    value = back[c] + matmul(ref["gout"][:, pl.ds(features, rank)], ref["down"][:, at])
                else:
                    from_mate = job["part"][c] is None
                    part = ref["extra"][:, pl.ds(features + len(extra[1]) * span, span)].astype(F32) if from_mate else ref[("part", j, c)][...]
                    value = back[c] + part
                if job["open"]:
                    ref[("out", ("open", j))][:, mine] = value
                else:
                    back_v[:, mine] = value.astype(BF16)
                    put(back_v.at[:, mine], ref[("out", "grad")].at[:, at])
        if sums is not None:
            span = jobs[0]["span"]
            chip, mine = lax.div(place[OWN], span), half_rows(place[0], span // 2)
            rest = cols(sums[4] + place[0] * lanes, lanes)
            value = ref[("sums", 0)][chip, mine, :] + ref[("sums", 1)][chip, mine, :].astype(F32)
            value = value + ref[("sums", 2)][:, rest].astype(F32) + ref[("sums", 3)][:, rest].astype(F32)
            value = (sums[5] * value).T
            ref[("out", ("sums", 0))][...] = value[: lanes // 2]
            ref[("out", ("sums", 1))][...] = value[lanes // 2 :]
        for copy in stores:
            copy.wait()

    result = call(
        kernel, args, specs, [shape for _, shape in outs], out_specs, scratch, aliases,
        weight=12, limit=STEP_LIMIT,
    )
    result = dict(zip(out_names, result))
    opened = [result[("open", j)] for j, job in enumerate(jobs) if job["open"]]
    if sums is not None:
        opened += [result[("sums", n)] for n in range(2)]
    return result.get("total", total), result.get("updated", updated), result.get("grad", grad_attn), *opened


class Part:
    def __init__(self, array, row=0, col=0):
        self.array, self.row, self.col = array, row, col


def span_of(jobs):
    sizes = []
    for job in jobs:
        some = job["pieces"][0][0]
        sizes.append(2 * some[0].shape[0] if isinstance(some, tuple) else some.shape[0])
    return min(sizes)


def job(chips, blocks, pieces, part=None, open=False, final=False, folded=False):
    return dict(chips=chips, blocks=blocks, pieces=pieces, part=part, open=open, final=final, folded=folded)


EDGES = dict(
    gout="s",
    k0="s",
    r1="T",
    x1="T",
    q1="rTm",
    s2="Tx",
    k2="x",
    r3="S",
    x3="S",
    q3="Tx",
    s3="Tx",
    k3="x",
    r4="TX",
    x4="s",
    q4="rT",
    send="r",
    q5="e",
)
WHEN = "srs"


def after(value, *others):
    return lax.optimization_barrier((value, *others))[0]


def ring_body(
    table,
    attn,
    resid,
    frozen,
    adapter_down_weight,
    adapter_up_weight,
    timestep_gate,
    guidance_gate,
    timestep_index,
    guidance_index,
    cotangent,
):
    rows, features = attn.shape
    axis_size = lax.axis_size("blk")
    chips = axis_size // 2
    blocks = blocks_of(features)
    me = lax.axis_index("blk")
    device = lax.axis_index("groups") * axis_size + me
    core_pairs = [(i, i ^ 1) for i in range(axis_size)]
    ring = functools.partial(lax.ppermute, axis_name="blk", perm=ring_pairs(chips))
    swap = functools.partial(lax.ppermute, axis_name="blk", perm=core_pairs)
    cross = functools.partial(lax.ppermute, axis_name="groups", perm=[(0, 1), (1, 0)])
    place = lax.dynamic_index_in_dim(jnp.asarray(table), device, 0, False)

    rank = adapter_up_weight.shape[0]
    steps = chips // 2 - 1
    far = near(steps + 1)
    wide = blocks[1]
    def gate(name, value, **have):
        others = [have[k] for k in EDGES.get(name, "") if have.get(k) is not None]
        return after(value, *others) if others else value

    theirs = swap(frozen)
    own = pair(place, cut(place, frozen, blocks), theirs, blocks, [0, 1, 2, 3])
    r, q, s = [None, ring(own[0])], [None], [None, ring(own[2])]
    known = dict(o=own[0], p=own[1], r=r[1], s=s[1])
    attn_t = known["a"] = swap(gate("attn", attn, **known))
    gate_row, gout, low, up, down_t, terms, given = adapter(
        place, timestep_index, guidance_index, attn, gate("adapter", cotangent, **known),
        adapter_down_weight.T, adapter_up_weight, timestep_gate, guidance_gate, blocks, chips,
    )
    terms_t = known["t"] = swap(given)
    first_q = known["f"] = chunk(place, far, own[1], wide, terms, terms_t, "first")
    q.append(ring(first_q))
    known["q"] = q[1]
    gout_t = known["m"] = swap(gate("gout", gout, **known))
    grads = (gout, down_t, rank)
    total, _, grad_attn = step(
        place, [job([OWN], [0, 1, 2, 3], [[block] for block in own])], attn, blocks,
        (gate("k0", gout, **known), down_t, rank), add=(low, up),
    )
    totals, parts, give, gives, x = (total, None), None, None, [], [None]

    def run(n, arrival, **have):
        nonlocal totals, parts, grad_attn, give
        last = n == steps
        totals, parts, grad_attn, give = side_step(
            place, n, attn, gate(f"k{n}", after(gout, arrival), **have), (attn_t, gout_t), down_t, rank, blocks,
            [r[n], q[n], s[n]], x[n - 1], totals, parts, grad_attn, gives, last,
        )
        if give is not None and not last:
            gives.append(give)

    for n in range(1, steps + 1):
        last = n == steps
        prev = dict(T=totals[0], x=x[n - 1], S=s[n - 1], Q=q[n - 1])
        r[n] = gate(f"r{n}", r[n], **{**known, **prev})
        r.append(ring(own_half(place, r[n]) if last else r[n]))
        x.append(cross(gate(f"x{n}", r[n], **prev)))
        if n > 1 and WHEN[n - 2] == "r":
            run(n - 1, r[n], x=x[n - 1], X=x[n - 2])
        q[n] = gate(f"q{n}", q[n], **{**known, "r": r[n], "T": totals[0], "x": x[n - 1]})
        if not last:
            message = chunk(place, across(steps + 1 - n), q[n], wide, terms, terms_t, "middle")
            q.append(ring(message))
        if n > 1 and WHEN[n - 2] == "q":
            run(n - 1, q[n], x=x[n - 1], X=x[n - 2], c=message)
        s[n] = gate(f"s{n}", s[n], **{**known, "q": q[n], "r": r[n], "T": totals[0], "x": x[n - 1]})
        if last:
            message = last_chunk(place, across(1), q[n], s[n], wide, terms, terms_t)
            q.append(ring(message))
        else:
            s.append(ring(s[n]))
        if WHEN[n - 1] == "s":
            run(n, s[n], x=x[n - 1], c=message)

    r_far = gate("r4", r[steps + 1], X=x[steps], T=totals[0], s=s[steps], q=q[steps])
    x_far = cross(gate("x4", r_far, X=x[steps], T=totals[0], s=s[steps]))
    if WHEN[steps - 1] == "r":
        run(steps, r_far, X=x[steps], c=message)
    x_before = gate("back", x[steps], r=r_far)
    x_swapped, r_swapped = swap(x_before), swap(r_far)
    swaps = dict(v=x_swapped, w=r_swapped)
    q_far = gate("q4", q[steps + 1], r=r_far, T=totals[0], **swaps)
    if WHEN[steps - 1] == "q":
        run(steps, q_far, X=x[steps], c=message)
    extra = swap(gate("send", give, r=r_far, X=x[steps], q=q_far))
    q_swapped = swap(gate("q5", q_far, e=extra, **swaps))
    x_job = job([near(steps), across(steps)], [3], [[x_before, x_swapped]], part=[parts[0], None], folded=True)
    q_piece, s_piece = (q_far, q_swapped), (Part(q_far, 0, wide), Part(q_swapped, 0, wide))
    columns = [across(n) for n in range(1, steps)]
    far_job = job([far], [0, 1, 2], [[(r_far, r_swapped)], [q_piece], [s_piece]], open=True, final=True)
    total, updated, grad_attn, part = step(
        place, [x_job, far_job], attn, blocks, grads, total=totals[0], final=(resid, gate_row), grad_attn=grad_attn,
        extra=(extra, columns),
    )
    x_far = gate("x5", x_far, s=q_far, q=q_far, T=total)
    sums = (terms, terms_t, q_far, q_swapped, wide + blocks[2], float(rows * axis_size) ** (-0.5))
    _, updated, grad_attn, grad_down_t, grad_up = step(
        place, [job([far], [3], [[(x_far, swap(x_far))]], part=[part], final=True, folded=True)],
        attn, blocks, grads, total=total, final=(resid, gate_row), updated=updated, grad_attn=grad_attn, sums=sums,
    )
    return updated, grad_attn, grad_down_t.T, grad_up.T


def gather_body(
    attn,
    resid,
    frozen,
    adapter_down_weight,
    adapter_up_weight,
    timestep_gate,
    guidance_gate,
    timestep_index,
    guidance_index,
    cotangent,
):
    rows, features = attn.shape
    axis_size = lax.axis_size("blk")
    whole = lax.all_gather(frozen, "blk", axis=0, tiled=True)
    sample = (lax.axis_index("blk") * rows + jnp.arange(rows, dtype=jnp.int32)) // IMAGE_TOKENS
    gate = timestep_gate[timestep_index[sample]] + guidance_gate[guidance_index[sample]]
    down_half = adapter_down_weight.astype(BF16)
    up_half = adapter_up_weight.astype(BF16)
    low = matmul(attn, down_half).astype(BF16)
    gout = (gate * cotangent.astype(F32)).astype(BF16)
    glow = contract_cols(gout, up_half).astype(BF16)
    terms = jnp.concatenate([contract_rows(attn, glow), contract_rows(gout, low)], 1)
    summed = lax.psum_scatter(terms, "blk", scatter_dimension=0, tiled=True)
    grad_scale = float(rows * axis_size) ** (-0.5)
    rank = glow.shape[1]
    base = matmul(attn, whole) + matmul(low, up_half)
    updated = (resid.astype(F32) + gate * base).astype(BF16)
    grad_attn = (contract_cols(gout, whole) + contract_cols(glow, down_half)).astype(BF16)
    return updated, grad_attn, grad_scale * summed[:, :rank], grad_scale * summed[:, rank:]


def solution(mesh):
    def run(attn, resid, frozen, *rest):
        axis_size, groups = mesh.shape["blk"], mesh.shape["groups"]
        rows, span = attn.shape[0] // (axis_size * groups), 2 * frozen.shape[0] // axis_size
        by_ring = groups == 2 and axis_size == 16
        by_ring = by_ring and span % 128 == 0 and frozen.shape[1] % 3072 == 0 and IMAGE_TOKENS % rows == 0
        body = gather_body
        if by_ring:
            table = place_table(groups, axis_size, rows, span, frozen.shape[1])
            body = functools.partial(ring_body, table)
        spec = P(("groups", "blk"), None)
        return jax.shard_map(
            body,
            mesh=mesh,
            in_specs=(spec, spec, P("blk", None), P(), P(), P(), P(), P("groups"), P("groups"), spec),
            out_specs=(spec, spec, spec, spec),
            check_vma=False,
        )(attn, resid, frozen, *rest)

    return run
```
